32 devices in a mesh: tok: 8 (over y, x, core), feat: 4 (over z).
Axes of the slice: x: 2, y: 2, z: 4, core: 2. Of those that a mesh axis runs over, the one named last changes fastest.
Arguments:
- calib: float32 [1280, 28672], P('tok', 'feat'), may hold values from -6 to 6
- weight: float32 [28672, 512], P('feat', 'tok'), may hold values from -0.03125 to 0.03125
Outputs:
- gram_product: float32 [512, 28672], P('tok', 'feat')
The draws below stay inside these ranges and needn't reach their ends.
All inputs are finite; a program needn't handle non-finite values.
Results may differ from the reference program's by a relative error of at most 0.000098.
Values sent between devices are 32-bit elements; how exact they have to be, the bound alone decides.
No kernel may reach another device: no remote copies, remote signals or barrier semaphores. Data moves between devices by JAX's collectives and lax.ppermute only.
A program may use at most 64 MiB of HBM per device.

```python
import math
import jax
import jax.numpy as jnp
from jax import lax

F = 28672
C = 512
TOKENS = 1280


def block_scale(stream_key, extent, shards, smallest, largest):
    def one(axis_at, shards_of):
        draws = jax.random.uniform(jax.random.fold_in(jax.random.fold_in(stream_key, 6), axis_at), (shards_of,), jnp.float32, smallest / len(shards), largest / len(shards))
        return jnp.repeat(jnp.exp(draws), extent[axis_at] // shards_of).reshape((-1,) + (1,) * (len(extent) - axis_at - 1))

    level = one(*shards[0])
    for cut in shards[1:]:
        level = level * one(*cut)
    return level


def gaussian(own_key, shape, scale, reach, cuts=(), kind=jnp.bfloat16):
    result = jax.random.normal(own_key, shape, jnp.float32) * scale
    if len(cuts) > 0:
        result = block_scale(own_key, shape, cuts, -0.22, 0.18) * result
    return jnp.clip(result, min=-reach, max=reach).astype(kind)


def setup_inputs(seed: int = 0) -> dict:
    splits = jax.random.split(jax.random.key(seed), 3)
    calib = gaussian(splits[0], (TOKENS, F), 1.0, 6.0, ((0, 8), (1, 4)), jnp.float32)
    weight = gaussian(splits[1], (F, C), F ** -0.5, 0.03125, ((0, 4), (1, 8)), jnp.float32)
    return dict(calib=calib, weight=weight)


def reference(calib, weight):
    mixed = jnp.dot(calib, weight, precision=lax.Precision.HIGHEST, preferred_element_type=jnp.float32)
    gram = lax.dot_general(mixed, calib, (((0,), (0,)), ((), ())), precision=lax.Precision.HIGHEST, preferred_element_type=jnp.float32)
    return gram * (1.0 / math.sqrt(TOKENS))
```

```python
import math

import jax
import jax.numpy as jnp
from jax import lax
from jax.sharding import PartitionSpec as P

CHUNKS = 2


def routes(side):
    place = lambda a, b, core: ((a % side) * side + b % side) * 2 + core
    every = [(a, b, core) for a in range(side) for b in range(side) for core in (0, 1)]

    def over(step, cross, lead):
        pairs = []
        for a, b, core in every:
            along_a = (core ^ cross if lead == "receiver" else core) == 0
            there = (a + step, b) if along_a else (a, b + step)
            pairs.append((place(a, b, core), place(*there, core ^ cross)))
        return pairs

    def rows(step, cross):
        pairs = []
        for a, b, core in every:
            along_b = core ^ cross == 0
            there = (a, b + step) if along_b else (a + step, b)
            pairs.append((place(a, b, core), place(*there, core ^ cross)))
        return pairs

    def columns(step, cross):
        return over(step, cross, "receiver")

    def results(step, cross):
        return over(step, cross, "sender")

    def swap(row, column):
        pairs = []
        for a, b, core in every:
            there = (a + column, b + row) if core == 0 else (a + row, b + column)
            pairs.append((place(a, b, core), place(*there, 1 - core)))
        return pairs

    return rows, columns, results, swap


def split(x):
    high = lax.reduce_precision(x, 8, 7)
    return high.astype(jnp.bfloat16), (x - high).astype(jnp.bfloat16)


def product(left, right, dims):
    (lh, ll), (rh, rl) = left, right
    dot = lambda l, r: lax.dot_general(
        l, r, (dims, ((), ())), preferred_element_type=jnp.float32
    )
    return dot(lh, rh) + (dot(lh, rl) + dot(ll, rh))


def shards(side, chunks, calib, weight):
    zs = lax.axis_size("feat")
    z = lax.axis_index("feat")
    core = lax.axis_index("tok") % 2
    tokens, features = calib.shape
    half = features // 2
    width = weight.shape[1] // chunks
    part = tokens // zs
    rows, columns, results, swap = routes(side)
    turns = range(side)
    send = lambda x, pairs: lax.ppermute(x, "tok", pairs)
    factor = 1.0 / math.sqrt(tokens * lax.axis_size("tok"))

    def halves(x):
        own = lax.dynamic_slice_in_dim(x, core * half, half, 1)
        other = lax.dynamic_slice_in_dim(x, (1 - core) * half, half, 1)
        return own, other

    def gather(x, route):
        own, other = halves(x)
        got = {(0, 0): own}
        for s in turns:
            if s:
                got[-s % side, 0] = send(own, route(s, 0))
            got[-s % side, 1] = send(other, route(s, 1))
        return jnp.concatenate([got[r, c] for r in turns for c in (0, 1)], 0)

    acts = split(gather(calib, rows))
    turned = weight.T
    pieces = []
    for j in range(chunks):
        cols = split(gather(turned[j * width : (j + 1) * width], columns))
        mixed = product(acts, cols, ((1,), (1,)))
        mixed = mixed.reshape(side * 2, zs, part, side * 2 * width)

        def piece(at):
            return lax.dynamic_index_in_dim(mixed, at % zs, 1, keepdims=False)

        shift = lambda s: [(i, (i + s) % zs) for i in range(zs)]
        total = piece(z)
        for s in range(1, zs):
            total = total + lax.ppermute(piece(z + s), "feat", shift(s))
        blocks = total.reshape(side, 2, part, side, 2, width)
        grid = [[None] * side for _ in turns]
        for r in turns:
            for q in turns:
                block = blocks[r, ::-1, :, q, ::-1].reshape(2 * part, 2 * width)
                block = send(block, swap(r, q)).reshape(2, part, 2, width)
                mine = blocks[-q % side, :, :, -r % side]
                grid[-q % side][-r % side] = mine + block
        total = jnp.stack([jnp.stack(g, 2) for g in grid], 0)
        total = total.reshape(side * 2, part, side * 2 * width) * factor
        got = [total] + [
            lax.ppermute(total, "feat", shift(s)) for s in range(zs - 1, 0, -1)
        ]
        ring = jnp.stack(got + got, 1)
        mixed = lax.dynamic_slice_in_dim(ring, (zs - z) % zs, zs, 1)
        mixed = split(mixed.reshape(side * 2 * tokens, side * 2 * width))
        term = product(mixed, acts, ((0,), (0,)))
        term = term.reshape(side, 2, width, half)
        own, other = term[0, 0], send(term[0, 1], results(0, 1))
        for s in turns[1:]:
            own = own + send(term[s, 0], results(s, 0))
            other = other + send(term[s, 1], results(s, 1))
        left = jnp.where(core == 0, own, other)
        right = jnp.where(core == 0, other, own)
        pieces.append(jnp.concatenate([left, right], 1))
    return jnp.concatenate(pieces, 0)


def solution(mesh):
    side = math.isqrt(mesh.shape["tok"] // 2)

    def step(calib, weight):
        return shards(side, CHUNKS, calib, weight)

    return jax.shard_map(
        step,
        mesh=mesh,
        in_specs=(P("tok", "feat"), P("feat", "tok")),
        out_specs=P("tok", "feat"),
        check_vma=False,
    )
```

```python
import functools
import math

import jax
import jax.numpy as jnp
from jax import lax
from jax.experimental import pallas as pl
from jax.experimental.pallas import tpu as pltpu
from jax.sharding import PartitionSpec as P

VMEM = pl.BlockSpec(memory_space=pltpu.VMEM)
PARAMS = pltpu.CompilerParams(vmem_limit_bytes=20 * 2**20)


def routes(side):
    place = lambda a, b, core: ((a % side) * side + b % side) * 2 + core
    every = [(a, b, core) for a in range(side) for b in range(side) for core in (0, 1)]

    def along(step, cross, which):
        pairs = []
        for a, b, core in every:
            moves_a = {"rows": core ^ cross == 1, "columns": core ^ cross == 0, "results": core == 0}
            there = (a + step, b) if moves_a[which] else (a, b + step)
            pairs.append((place(a, b, core), place(*there, core ^ cross)))
        return pairs

    def swap(row, column):
        pairs = []
        for a, b, core in every:
            there = (a + column, b + row) if core == 0 else (a + row, b + column)
            pairs.append((place(a, b, core), place(*there, 1 - core)))
        return pairs

    return along, swap


def split(x):
    high = x.astype(jnp.bfloat16)
    return high, (x - high.astype(jnp.float32)).astype(jnp.bfloat16)


def dot(left, right):
    return jnp.dot(left, right, preferred_element_type=jnp.float32)


def block_of(size, most):
    return next(b for b in range(most, 0, -128) if size % b == 0)


def cut_kernel(cuts, calib, turned, *refs):
    outs, sems = refs[:-1], refs[-1]
    half = turned.shape[1] // 2
    core = lax.axis_index("tok") & 1
    copies = []
    for source, start, size in [(turned, 0, turned.shape[0])] + [(calib, *cut) for cut in cuts]:
        for first in (1 - core, core):
            at = pl.ds(pl.multiple_of(first * half, half), half)
            k = len(copies)
            copy = pltpu.make_async_copy(
                source.at[pl.ds(start, size), at], outs[k], sems.at[k]
            )
            copy.start()
            copies.append(copy)
    for copy in copies:
        copy.wait()


def cut(calib, turned, cuts):
    half = calib.shape[1] // 2
    sizes = [turned.shape[0]] + [size for _, size in cuts]
    return pl.pallas_call(
        functools.partial(cut_kernel, cuts),
        out_shape=[jax.ShapeDtypeStruct((n, half), jnp.float32) for n in sizes for _ in range(2)],
        in_specs=[pl.BlockSpec(memory_space=pltpu.HBM)] * 2,
        out_specs=[VMEM] * (2 * len(sizes)),
        scratch_shapes=[pltpu.SemaphoreType.DMA((2 * len(sizes),))],
        compiler_params=PARAMS,
        name="cut",
    )(calib, turned)


def turn_kernel(*refs):
    inputs, out = refs[:-1], refs[-1]
    width, half = inputs[0].shape
    columns = width * len(inputs)
    step = block_of(half, 512)

    @pl.loop(0, half // step)
    def _(i):
        at = pl.ds(pl.multiple_of(i * step, step), step)
        x = jnp.concatenate([ref[:, at] for ref in inputs], 0).T
        out[at, :columns], out[at, columns:] = split(x)


def turn(inputs):
    width, half = inputs[0].shape
    return pl.pallas_call(
        turn_kernel,
        out_shape=jax.ShapeDtypeStruct((half, 2 * width * len(inputs)), jnp.bfloat16),
        in_specs=[VMEM] * len(inputs),
        out_specs=VMEM,
        compiler_params=PARAMS,
        name="turn",
    )(*inputs)


def mix_kernel(count, zs, *refs):
    inputs, cols = refs[:count], refs[count]
    pieces, (high, low), acc = refs[count + 1 : count + 1 + zs], refs[-3:-1], refs[-1]
    half = inputs[0].shape[1]
    width = acc.shape[1]
    z = lax.axis_index("feat")
    step = block_of(half, 1024)
    acc[...] = jnp.zeros(acc.shape, jnp.float32)

    @pl.loop(0, half // step)
    def _(i):
        at = pl.ds(pl.multiple_of(i * step, step), step)
        h, l = split(jnp.concatenate([x[:, at] for x in inputs], 0))
        high[:, at], low[:, at] = h, l
        w = cols[at, :]
        d = dot(h, w)
        acc[...] += d[:, :width] + (d[:, width:] + dot(l, w[:, :width]))

    first = 0
    for x in inputs:
        part = x.shape[0] // zs
        for s in range(zs):
            pieces[s][first // zs : first // zs + part] = acc[pl.ds(first + (z ^ s) * part, part)]
        first += x.shape[0]


def mix(inputs, cols, zs):
    count, half = len(inputs), inputs[0].shape[1]
    rows = sum(x.shape[0] for x in inputs)
    width = cols.shape[1] // 2
    act = jax.ShapeDtypeStruct((rows, half), jnp.bfloat16)
    piece = jax.ShapeDtypeStruct((rows // zs, width), jnp.float32)
    outs = pl.pallas_call(
        functools.partial(mix_kernel, count, zs),
        out_shape=[piece] * zs + [act] * 2,
        in_specs=[VMEM] * (count + 1),
        out_specs=[VMEM] * (zs + 2),
        scratch_shapes=[pltpu.VMEM((rows, width), jnp.float32)],
        compiler_params=PARAMS,
        cost_estimate=pl.CostEstimate(
            flops=6 * rows * half * width,
            bytes_accessed=8 * rows * half + 4 * half * width,
            transcendentals=0,
        ),
        name="mix",
    )(*inputs, cols)
    return outs[:zs], outs[zs:]


def pack_kernel(side, zs, moves, *refs):
    total, outs = refs[len(moves) * zs], refs[len(moves) * zs + 1 :]
    rows, columns = total.shape
    head = rows // side
    part, width = head // 2, columns // side // 2
    for k, segments in enumerate(moves):
        got = refs[k * zs : (k + 1) * zs]
        for start, size, to in segments:
            x = got[0][start : start + size]
            for g in got[1:]:
                x = x + g[start : start + size]
            total[to : to + size] = x
    for r in range(side):
        for q in range(side):
            out = outs[r * side + q]
            for e in (0, 1):
                a = r * head + (1 - e) * part
                x = total[a : a + part, 2 * q * width : 2 * (q + 1) * width]
                out[e * part : (e + 1) * part] = jnp.concatenate([x[:, width:], x[:, :width]], 1)


def pack(side, groups, moves):
    zs, columns = len(groups[0]), groups[0][0].shape[1]
    rows = sum(group[0].shape[0] for group in groups)
    block = jax.ShapeDtypeStruct((rows // side, columns // side), jnp.float32)
    outs = pl.pallas_call(
        functools.partial(pack_kernel, side, zs, moves),
        out_shape=[jax.ShapeDtypeStruct((rows, columns), jnp.float32)] + [block] * side**2,
        in_specs=[VMEM] * (len(moves) * zs),
        out_specs=[VMEM] * (1 + side**2),
        compiler_params=PARAMS,
        name="pack",
    )(*[x for group in groups for x in group])
    return outs[0], outs[1:]


def merge_kernel(side, factor, qs, count, *refs):
    out = refs[-1]
    first = 0
    for c in range(count):
        total, *got = refs[c * (1 + side * len(qs)) : (c + 1) * (1 + side * len(qs))]
        head, width = got[0].shape
        for i, q in enumerate(qs):
            for r in range(side):
                x = total[r * head : (r + 1) * head, q * width : (q + 1) * width]
                x = (x + got[i * side + r][...]) * factor
                out[first + r * head : first + (r + 1) * head, i * width : (i + 1) * width] = x
        first += total.shape[0]


def merge(side, factor, qs, chunks):
    inputs = []
    for total, got in chunks:
        inputs += [total] + [got[(-q % side) * side + -r % side] for q in qs for r in range(side)]
    rows = sum(total.shape[0] for total, _ in chunks)
    columns = chunks[0][0].shape[1] // side * len(qs)
    return pl.pallas_call(
        functools.partial(merge_kernel, side, factor, qs, len(chunks)),
        out_shape=jax.ShapeDtypeStruct((rows, columns), jnp.float32),
        in_specs=[VMEM] * len(inputs),
        out_specs=VMEM,
        compiler_params=PARAMS,
        name="merge",
    )(*inputs)


def term_kernel(zs, spots, groups, *refs):
    got = [refs[c * zs : (c + 1) * zs] for c in range(len(spots))]
    refs = refs[len(spots) * zs :]
    acts = refs[: 2 * groups]
    outs, full = refs[2 * groups : -1], refs[-1]
    columns = full.shape[1]
    width, half = outs[0].shape
    z = lax.axis_index("feat")
    for pieces, segments in zip(got, spots):
        for s in range(zs):
            for at, part, to in segments:
                full[pl.ds(to + (z ^ s) * part, part)] = pieces[s][at : at + part]
    h, l = split(full[...].T)
    both = jnp.concatenate([h, l], 0)
    step = block_of(half, 512)

    @pl.loop(0, half // step)
    def _(i):
        at = pl.ds(pl.multiple_of(i * step, step), step)
        high = jnp.concatenate([x[:, at] for x in acts[::2]], 0)
        low = jnp.concatenate([x[:, at] for x in acts[1::2]], 0)
        d = dot(both, high)
        total = d[:columns] + (d[columns:] + dot(h, low))
        for o, out in enumerate(outs):
            out[:, at] = total[o * width : (o + 1) * width]


def terms(got, acts, spots, width, cost=1):
    zs, columns = len(got[0]), got[0][0].shape[1]
    half = acts[0][0].shape[1]
    count = columns // width
    rows = sum(act[0].shape[0] for act in acts)
    return pl.pallas_call(
        functools.partial(term_kernel, zs, spots, len(acts)),
        out_shape=[jax.ShapeDtypeStruct((width, half), jnp.float32)] * count,
        in_specs=[VMEM] * (zs * len(got) + 2 * len(acts)),
        out_specs=[VMEM] * count,
        scratch_shapes=[pltpu.VMEM((rows, columns), jnp.float32)],
        compiler_params=PARAMS,
        cost_estimate=pl.CostEstimate(
            flops=cost * 6 * rows * columns * half,
            bytes_accessed=cost * (4 * rows * half + 4 * columns * half),
            transcendentals=0,
        ),
        name="term",
    )(*[x for pieces in got for x in pieces], *[x for act in acts for x in act])


def join_kernel(count, *refs):
    out = refs[-1]
    core = lax.axis_index("tok") & 1
    half = out.shape[1] // 2
    for side, at in ((refs[:count], core), (refs[count : 2 * count], 1 - core)):
        total = side[0][...]
        for x in side[1:]:
            total = total + x[...]
        out[:, pl.ds(pl.multiple_of(at * half, half), half)] = total


def arrived_kernel(*refs):
    refs[-1][...] = jnp.zeros_like(refs[-1])


def arrived(blocks):
    return pl.pallas_call(
        arrived_kernel,
        out_shape=jax.ShapeDtypeStruct((8, 128), jnp.float32),
        in_specs=[pl.BlockSpec(memory_space=pl.ANY)] * len(blocks),
        out_specs=VMEM,
        compiler_params=PARAMS,
        cost_estimate=pl.CostEstimate(flops=10**10, bytes_accessed=0, transcendentals=0),
        name="arrived",
    )(*blocks)


def join(own, other, mark):
    width, half = own[0].shape
    rows = 16 if width % 16 == 0 else width
    return pl.pallas_call(
        functools.partial(join_kernel, len(own)),
        grid=(width // rows,),
        out_shape=jax.ShapeDtypeStruct((width, 2 * half), jnp.float32),
        in_specs=[pl.BlockSpec((rows, half), lambda i: (i, 0))] * (2 * len(own))
        + [pl.BlockSpec(memory_space=pl.ANY)],
        out_specs=pl.BlockSpec((rows, 2 * half), lambda i: (i, 0)),
        compiler_params=PARAMS,
        name="join",
    )(*own, *other, mark)


def shards(side, calib, weight):
    zs = lax.axis_size("feat")
    tokens = calib.shape[0]
    width = weight.shape[1]
    along, swap = routes(side)
    turns = range(side)
    send = lambda x, pairs: lax.ppermute(x, "tok", pairs)
    across = lambda x, s: lax.ppermute(x, "feat", [(i, i ^ s) for i in range(zs)])
    factor = 1.0 / math.sqrt(tokens * lax.axis_size("tok"))
    unit = 8 * zs if tokens % (8 * zs) == 0 else zs
    late = unit * max(1, tokens // unit * 2 // 5)
    sizes = [tokens - late, late]

    def reduce(group, cols):
        pieces, act = mix(group, cols, zs)
        return list(pieces[:1]) + [across(pieces[s], s) for s in order][::-1], act

    order = range(zs - 1, 0, -1)

    def far(own, other, which):
        got = []
        for r in turns[1:]:
            got.append(send(own, along(side - r, 0, which)))
            got.append(send(other, along(side - r, 1, which)))
        return got

    cuts = [(0, sizes[0]), (sizes[0], sizes[1])]
    parts = cut(calib, weight.T, cuts)
    other, own = parts[:2]
    cols = turn([own, send(other, along(0, 1, "columns"))] + far(own, other, "columns"))
    near = []
    for c in (0, 1):
        other, own = parts[2 + 2 * c : 4 + 2 * c]
        near += [own, send(other, along(0, 1, "rows"))]
    hold = lax.optimization_barrier
    last, act = reduce(near, cols)
    acts, groups = [act], [last]
    for other, own in (parts[2:4], parts[4:6]):
        group, groups[-1] = hold((far(own, other, "rows"), groups[-1]))
        last, act = reduce(group, cols)
        acts.append(act)
        groups.append(last)

    part, first = tokens // zs, 2 * tokens
    moves, spots = [[], [], []], []
    for c in (0, 1):
        size = sizes[c] // zs
        for p in range(2 * side):
            at = p * part + c * sizes[0] // zs
            if p < 2:
                start = 2 * c * sizes[0] + p * sizes[c]
                moves[0].append((start // zs, size, at))
            else:
                start = first + (p - 2) * sizes[c]
                moves[c + 1].append(((p - 2) * size, size, at))
            spots.append((at, size, start))
        first += (2 * side - 2) * sizes[c]

    total, payloads = pack(side, groups, moves)
    pairs = [swap(r, q) for r in turns for q in turns]
    chunk = (total, [send(x, pair) for x, pair in zip(payloads, pairs)])

    def spread(mine):
        return [mine] + [across(mine, s) for s in order][::-1]

    away = spread(merge(side, factor, turns[1:], [chunk]))
    here = merge(side, factor, turns[:1], [chunk])
    here, away = hold((here, away))
    term = terms([away], acts, [spots], width, 0)
    same = [send(term[2 * q - 2], along(q, 0, "results")) for q in turns[1:]]
    cross = [send(term[2 * q - 1], along(q, 1, "results")) for q in turns[1:]]
    here = spread(here)
    here, term = hold((here, term))
    mine, near = terms([here], acts, [spots], width, 0)
    near = send(near, along(0, 1, "results"))
    return join([mine] + same, [near] + cross, arrived(same + cross))


def solution(mesh):
    side = math.isqrt(mesh.shape["tok"] // 2)

    def step(calib, weight):
        return shards(side, calib, weight)

    return jax.shard_map(
        step,
        mesh=mesh,
        in_specs=(P("tok", "feat"), P("feat", "tok")),
        out_specs=P("tok", "feat"),
        check_vma=False,
    )
```

```python
import functools
import math

import jax
import jax.numpy as jnp
from jax import lax
from jax.experimental import pallas as pl
from jax.experimental.pallas import tpu as pltpu
from jax.sharding import PartitionSpec as P

VMEM = pl.BlockSpec(memory_space=pltpu.VMEM)
PARAMS = pltpu.CompilerParams(vmem_limit_bytes=20 * 2**20)


def routes(side):
    place = lambda a, b, core: ((a % side) * side + b % side) * 2 + core
    every = [(a, b, core) for a in range(side) for b in range(side) for core in (0, 1)]

    def along(step, cross, which):
        pairs = []
        for a, b, core in every:
            moves_a = {"rows": core ^ cross == 1, "columns": core ^ cross == 0, "results": core == 0}
            there = (a + step, b) if moves_a[which] else (a, b + step)
            pairs.append((place(a, b, core), place(*there, core ^ cross)))
        return pairs

    def swap(row, column):
        pairs = []
        for a, b, core in every:
            there = (a + column, b + row) if core == 0 else (a + row, b + column)
            pairs.append((place(a, b, core), place(*there, 1 - core)))
        return pairs

    return along, swap


def split(x):
    high = x.astype(jnp.bfloat16)
    return high, (x - high.astype(jnp.float32)).astype(jnp.bfloat16)


def dot(left, right):
    return jnp.dot(left, right, preferred_element_type=jnp.float32)


def block_of(size, most):
    return next(b for b in range(most, 0, -128) if size % b == 0)


def cut_kernel(cuts, source, *refs):
    outs, sems = refs[:-1], refs[-1]
    half = source.shape[1] // 2
    core = lax.axis_index("tok") & 1
    copies = []
    for start, size in cuts:
        for first in (1 - core, core):
            at = pl.ds(pl.multiple_of(first * half, half), half)
            k = len(copies)
            copy = pltpu.make_async_copy(
                source.at[pl.ds(start, size), at], outs[k], sems.at[k]
            )
            copy.start()
            copies.append(copy)
    for copy in copies:
        copy.wait()


def cut(source, cuts):
    half = source.shape[1] // 2
    outs = pl.pallas_call(
        functools.partial(cut_kernel, cuts),
        out_shape=[jax.ShapeDtypeStruct((n, half), jnp.float32) for _, n in cuts for _ in range(2)],
        in_specs=[pl.BlockSpec(memory_space=pl.ANY)],
        out_specs=[VMEM] * (2 * len(cuts)),
        scratch_shapes=[pltpu.SemaphoreType.DMA((2 * len(cuts),))],
        compiler_params=PARAMS,
        name="cut",
    )(source)
    return [(outs[2 * i + 1], outs[2 * i]) for i in range(len(cuts))]


def turn_kernel(*refs):
    inputs, out = refs[:-1], refs[-1]
    width, half = inputs[0].shape
    columns = width * len(inputs)
    step = block_of(half, 512)

    @pl.loop(0, half // step)
    def _(i):
        at = pl.ds(pl.multiple_of(i * step, step), step)
        x = jnp.concatenate([ref[:, at] for ref in inputs], 0).T
        out[at, :columns], out[at, columns:] = split(x)


def turn(inputs):
    width, half = inputs[0].shape
    return pl.pallas_call(
        turn_kernel,
        out_shape=jax.ShapeDtypeStruct((half, 2 * width * len(inputs)), jnp.bfloat16),
        in_specs=[VMEM] * len(inputs),
        out_specs=VMEM,
        compiler_params=PARAMS,
        name="turn",
    )(*inputs)


def mix_kernel(count, zs, *refs):
    inputs, cols = refs[:count], refs[count]
    pieces, (high, low), acc = refs[count + 1 : count + 1 + zs], refs[-3:-1], refs[-1]
    half = inputs[0].shape[1]
    width = acc.shape[1]
    z = lax.axis_index("feat")
    step = block_of(half, 1024)
    acc[...] = jnp.zeros(acc.shape, jnp.float32)

    @pl.loop(0, half // step)
    def _(i):
        at = pl.ds(pl.multiple_of(i * step, step), step)
        h, l = split(jnp.concatenate([x[:, at] for x in inputs], 0))
        high[:, at], low[:, at] = h, l
        w = cols[at, :]
        d = dot(h, w)
        acc[...] += d[:, :width] + (d[:, width:] + dot(l, w[:, :width]))

    first = 0
    for x in inputs:
        part = x.shape[0] // zs
        for s in range(zs):
            pieces[s][first // zs : first // zs + part] = acc[pl.ds(first + (z ^ s) * part, part)]
        first += x.shape[0]


def mix(inputs, cols, zs):
    count, half = len(inputs), inputs[0].shape[1]
    rows = sum(x.shape[0] for x in inputs)
    width = cols.shape[1] // 2
    act = jax.ShapeDtypeStruct((rows, half), jnp.bfloat16)
    piece = jax.ShapeDtypeStruct((rows // zs, width), jnp.float32)
    outs = pl.pallas_call(
        functools.partial(mix_kernel, count, zs),
        out_shape=[piece] * zs + [act] * 2,
        in_specs=[VMEM] * (count + 1),
        out_specs=[VMEM] * (zs + 2),
        scratch_shapes=[pltpu.VMEM((rows, width), jnp.float32)],
        compiler_params=PARAMS,
        cost_estimate=pl.CostEstimate(
            flops=6 * rows * half * width,
            bytes_accessed=8 * rows * half + 4 * half * width,
            transcendentals=0,
        ),
        name="mix",
    )(*inputs, cols)
    return outs[:zs], outs[zs:]


def pack_kernel(side, zs, moves, *refs):
    total, outs = refs[len(moves) * zs], refs[len(moves) * zs + 1 :]
    rows, columns = total.shape
    head = rows // side
    part, width = head // 2, columns // side // 2
    for k, segments in enumerate(moves):
        got = refs[k * zs : (k + 1) * zs]
        for start, size, to in segments:
            x = got[0][start : start + size]
            for g in got[1:]:
                x = x + g[start : start + size]
            total[to : to + size] = x
    for r in range(side):
        for q in range(side):
            out = outs[r * side + q]
            for e in (0, 1):
                a = r * head + (1 - e) * part
                x = total[a : a + part, 2 * q * width : 2 * (q + 1) * width]
                out[e * part : (e + 1) * part] = jnp.concatenate([x[:, width:], x[:, :width]], 1)


def pack(side, groups, moves):
    zs, columns = len(groups[0]), groups[0][0].shape[1]
    rows = sum(group[0].shape[0] for group in groups)
    block = jax.ShapeDtypeStruct((rows // side, columns // side), jnp.float32)
    outs = pl.pallas_call(
        functools.partial(pack_kernel, side, zs, moves),
        out_shape=[jax.ShapeDtypeStruct((rows, columns), jnp.float32)] + [block] * side**2,
        in_specs=[VMEM] * (len(moves) * zs),
        out_specs=[VMEM] * (1 + side**2),
        compiler_params=PARAMS,
        name="pack",
    )(*[x for group in groups for x in group])
    return outs[0], outs[1:]


def merge_kernel(side, factor, qs, count, *refs):
    out = refs[-1]
    first = 0
    for c in range(count):
        total, *got = refs[c * (1 + side * len(qs)) : (c + 1) * (1 + side * len(qs))]
        head, width = got[0].shape
        for i, q in enumerate(qs):
            for r in range(side):
                x = total[r * head : (r + 1) * head, q * width : (q + 1) * width]
                x = (x + got[i * side + r][...]) * factor
                out[first + r * head : first + (r + 1) * head, i * width : (i + 1) * width] = x
        first += total.shape[0]


def merge(side, factor, qs, chunks):
    inputs = []
    for total, got in chunks:
        inputs += [total] + [got[(-q % side) * side + -r % side] for q in qs for r in range(side)]
    rows = sum(total.shape[0] for total, _ in chunks)
    columns = chunks[0][0].shape[1] // side * len(qs)
    return pl.pallas_call(
        functools.partial(merge_kernel, side, factor, qs, len(chunks)),
        out_shape=jax.ShapeDtypeStruct((rows, columns), jnp.float32),
        in_specs=[VMEM] * len(inputs),
        out_specs=VMEM,
        compiler_params=PARAMS,
        name="merge",
    )(*inputs)


def term_kernel(zs, spots, groups, *refs):
    got = [refs[c * zs : (c + 1) * zs] for c in range(len(spots))]
    refs = refs[len(spots) * zs :]
    acts = refs[: 2 * groups]
    outs, full = refs[2 * groups : -1], refs[-1]
    columns = full.shape[1]
    width, half = outs[0].shape
    z = lax.axis_index("feat")
    for pieces, segments in zip(got, spots):
        for s in range(zs):
            for at, part, to in segments:
                full[pl.ds(to + (z ^ s) * part, part)] = pieces[s][at : at + part]
    h, l = split(full[...].T)
    both = jnp.concatenate([h, l], 0)
    step = block_of(half, 512)

    @pl.loop(0, half // step)
    def _(i):
        at = pl.ds(pl.multiple_of(i * step, step), step)
        high = jnp.concatenate([x[:, at] for x in acts[::2]], 0)
        low = jnp.concatenate([x[:, at] for x in acts[1::2]], 0)
        d = dot(both, high)
        total = d[:columns] + (d[columns:] + dot(h, low))
        for o, out in enumerate(outs):
            out[:, at] = total[o * width : (o + 1) * width]


def terms(got, acts, spots, width, cost=1):
    zs, columns = len(got[0]), got[0][0].shape[1]
    half = acts[0][0].shape[1]
    count = columns // width
    rows = sum(act[0].shape[0] for act in acts)
    return pl.pallas_call(
        functools.partial(term_kernel, zs, spots, len(acts)),
        out_shape=[jax.ShapeDtypeStruct((width, half), jnp.float32)] * count,
        in_specs=[VMEM] * (zs * len(got) + 2 * len(acts)),
        out_specs=[VMEM] * count,
        scratch_shapes=[pltpu.VMEM((rows, columns), jnp.float32)],
        compiler_params=PARAMS,
        cost_estimate=pl.CostEstimate(
            flops=cost * 6 * rows * columns * half,
            bytes_accessed=cost * (4 * rows * half + 4 * columns * half),
            transcendentals=0,
        ),
        name="term",
    )(*[x for pieces in got for x in pieces], *[x for act in acts for x in act])


def join_kernel(count, *refs):
    out = refs[-1]
    core = lax.axis_index("tok") & 1
    half = out.shape[1] // 2
    for side, at in ((refs[:count], core), (refs[count : 2 * count], 1 - core)):
        total = side[0][...]
        for x in side[1:]:
            total = total + x[...]
        out[:, pl.ds(pl.multiple_of(at * half, half), half)] = total


def arrived_kernel(*refs):
    refs[-1][...] = jnp.zeros_like(refs[-1])


def arrived(blocks):
    return pl.pallas_call(
        arrived_kernel,
        out_shape=jax.ShapeDtypeStruct((8, 128), jnp.float32),
        in_specs=[pl.BlockSpec(memory_space=pl.ANY)] * len(blocks),
        out_specs=VMEM,
        compiler_params=PARAMS,
        cost_estimate=pl.CostEstimate(flops=10**10, bytes_accessed=0, transcendentals=0),
        name="arrived",
    )(*blocks)


def join(own, other, mark):
    width, half = own[0].shape
    rows = 16 if width % 16 == 0 else width
    return pl.pallas_call(
        functools.partial(join_kernel, len(own)),
        grid=(width // rows,),
        out_shape=jax.ShapeDtypeStruct((width, 2 * half), jnp.float32),
        in_specs=[pl.BlockSpec((rows, half), lambda i: (i, 0))] * (2 * len(own))
        + [pl.BlockSpec(memory_space=pl.ANY)],
        out_specs=pl.BlockSpec((rows, 2 * half), lambda i: (i, 0)),
        compiler_params=PARAMS,
        name="join",
    )(*own, *other, mark)


def shards(side, calib, weight):
    zs = lax.axis_size("feat")
    tokens = calib.shape[0]
    width = weight.shape[1]
    along, swap = routes(side)
    turns = range(side)
    send = lambda x, pairs: lax.ppermute(x, "tok", pairs)
    across = lambda x, s: lax.ppermute(x, "feat", [(i, i ^ s) for i in range(zs)])
    factor = 1.0 / math.sqrt(tokens * lax.axis_size("tok"))
    unit = 8 * zs if tokens % (8 * zs) == 0 else zs
    late = unit * max(1, tokens // unit * 2 // 5)
    sizes = [tokens - late, late]

    def reduce(group, cols):
        pieces, act = mix(group, cols, zs)
        return list(pieces[:1]) + [across(pieces[s], s) for s in order][::-1], act

    order = range(zs - 1, 0, -1)

    def far(own, other, which):
        got = []
        for r in turns[1:]:
            got.append(send(own, along(side - r, 0, which)))
            got.append(send(other, along(side - r, 1, which)))
        return got

    ((own, other),) = cut(weight.T, [(0, width)])
    close = send(other, along(0, 1, "columns"))
    cols = turn([own, close] + far(own, other, "columns"))
    parts = [own, other]
    for own, other in cut(calib, [(0, sizes[0]), (sizes[0], sizes[1])]):
        parts += [other, own]
    near = []
    for c in (0, 1):
        other, own = parts[2 + 2 * c : 4 + 2 * c]
        near += [own, send(other, along(0, 1, "rows"))]
    hold = lax.optimization_barrier
    last, act = reduce(near, cols)
    acts, groups = [act], [last]
    for other, own in (parts[2:4], parts[4:6]):
        group, groups[-1] = hold((far(own, other, "rows"), groups[-1]))
        last, act = reduce(group, cols)
        acts.append(act)
        groups.append(last)

    part, first = tokens // zs, 2 * tokens
    moves, spots = [[], [], []], []
    for c in (0, 1):
        size = sizes[c] // zs
        for p in range(2 * side):
            at = p * part + c * sizes[0] // zs
            if p < 2:
                start = 2 * c * sizes[0] + p * sizes[c]
                moves[0].append((start // zs, size, at))
            else:
                start = first + (p - 2) * sizes[c]
                moves[c + 1].append(((p - 2) * size, size, at))
            spots.append((at, size, start))
        first += (2 * side - 2) * sizes[c]

    total, payloads = pack(side, groups, moves)
    pairs = [swap(r, q) for r in turns for q in turns]
    chunk = (total, [send(x, pair) for x, pair in zip(payloads, pairs)])

    def spread(mine):
        return [mine] + [across(mine, s) for s in order][::-1]

    away = spread(merge(side, factor, turns[1:], [chunk]))
    here = merge(side, factor, turns[:1], [chunk])
    here, away = hold((here, away))
    term = terms([away], acts, [spots], width, 0)
    same = [send(term[2 * q - 2], along(q, 0, "results")) for q in turns[1:]]
    cross = [send(term[2 * q - 1], along(q, 1, "results")) for q in turns[1:]]
    here = spread(here)
    here, term = hold((here, term))
    mine, near = terms([here], acts, [spots], width, 0)
    near = send(near, along(0, 1, "results"))
    return join([mine] + same, [near] + cross, arrived(same + cross))


def solution(mesh):
    side = math.isqrt(mesh.shape["tok"] // 2)

    def step(calib, weight):
        return shards(side, calib, weight)

    return jax.shard_map(
        step,
        mesh=mesh,
        in_specs=(P("tok", "feat"), P("feat", "tok")),
        out_specs=P("tok", "feat"),
        check_vma=False,
    )
```

```python
import functools
import math

import jax
import jax.numpy as jnp
from jax import lax
from jax.experimental import pallas as pl
from jax.experimental.pallas import tpu as pltpu
from jax.sharding import PartitionSpec as P

VMEM = pl.BlockSpec(memory_space=pltpu.VMEM)
PARAMS = pltpu.CompilerParams(vmem_limit_bytes=20 * 2**20)


def routes(side):
    place = lambda a, b, core: ((a % side) * side + b % side) * 2 + core
    every = [(a, b, core) for a in range(side) for b in range(side) for core in (0, 1)]

    def along(step, cross, which):
        pairs = []
        for a, b, core in every:
            moves_a = {"rows": core ^ cross == 1, "columns": core ^ cross == 0, "results": core == 0}
            there = (a + step, b) if moves_a[which] else (a, b + step)
            pairs.append((place(a, b, core), place(*there, core ^ cross)))
        return pairs

    def swap(row, column):
        pairs = []
        for a, b, core in every:
            there = (a + column, b + row) if core == 0 else (a + row, b + column)
            pairs.append((place(a, b, core), place(*there, 1 - core)))
        return pairs

    return along, swap


def split(x):
    high = x.astype(jnp.bfloat16)
    return high, (x - high.astype(jnp.float32)).astype(jnp.bfloat16)


def dot(left, right):
    return jnp.dot(left, right, preferred_element_type=jnp.float32)


def block_of(size, most):
    return next(b for b in range(most, 0, -128) if size % b == 0)


def cut_kernel(cuts, source, *refs):
    outs, sems = refs[:-1], refs[-1]
    half = source.shape[1] // 2
    core = lax.axis_index("tok") & 1
    copies = []
    for start, size in cuts:
        for first in (1 - core, core):
            at = pl.ds(pl.multiple_of(first * half, half), half)
            k = len(copies)
            copy = pltpu.make_async_copy(
                source.at[pl.ds(start, size), at], outs[k], sems.at[k]
            )
            copy.start()
            copies.append(copy)
    for copy in copies:
        copy.wait()


def cut(source, cuts):
    half = source.shape[1] // 2
    outs = pl.pallas_call(
        functools.partial(cut_kernel, cuts),
        out_shape=[jax.ShapeDtypeStruct((n, half), jnp.float32) for _, n in cuts for _ in range(2)],
        in_specs=[pl.BlockSpec(memory_space=pl.ANY)],
        out_specs=[VMEM] * (2 * len(cuts)),
        scratch_shapes=[pltpu.SemaphoreType.DMA((2 * len(cuts),))],
        compiler_params=PARAMS,
        name="cut",
    )(source)
    return [(outs[2 * i + 1], outs[2 * i]) for i in range(len(cuts))]


def turn_kernel(*refs):
    inputs, out = refs[:-1], refs[-1]
    width, half = inputs[0].shape
    columns = width * len(inputs)
    step = block_of(half, 512)

    @pl.loop(0, half // step)
    def _(i):
        at = pl.ds(pl.multiple_of(i * step, step), step)
        x = jnp.concatenate([ref[:, at] for ref in inputs], 0).T
        out[at, :columns], out[at, columns:] = split(x)


def turn(inputs):
    width, half = inputs[0].shape
    return pl.pallas_call(
        turn_kernel,
        out_shape=jax.ShapeDtypeStruct((half, 2 * width * len(inputs)), jnp.bfloat16),
        in_specs=[VMEM] * len(inputs),
        out_specs=VMEM,
        compiler_params=PARAMS,
        name="turn",
    )(*inputs)


def mix_kernel(count, zs, *refs):
    inputs, cols = refs[:count], refs[count]
    pieces, (high, low), acc = refs[count + 1 : count + 1 + zs], refs[-3:-1], refs[-1]
    half = inputs[0].shape[1]
    width = acc.shape[1]
    z = lax.axis_index("feat")
    step = block_of(half, 1024)
    acc[...] = jnp.zeros(acc.shape, jnp.float32)

    @pl.loop(0, half // step)
    def _(i):
        at = pl.ds(pl.multiple_of(i * step, step), step)
        h, l = split(jnp.concatenate([x[:, at] for x in inputs], 0))
        high[:, at], low[:, at] = h, l
        w = cols[at, :]
        d = dot(h, w)
        acc[...] += d[:, :width] + (d[:, width:] + dot(l, w[:, :width]))

    first = 0
    for x in inputs:
        part = x.shape[0] // zs
        for s in range(zs):
            pieces[s][first // zs : first // zs + part] = acc[pl.ds(first + (z ^ s) * part, part)]
        first += x.shape[0]


def mix(inputs, cols, zs):
    count, half = len(inputs), inputs[0].shape[1]
    rows = sum(x.shape[0] for x in inputs)
    width = cols.shape[1] // 2
    act = jax.ShapeDtypeStruct((rows, half), jnp.bfloat16)
    piece = jax.ShapeDtypeStruct((rows // zs, width), jnp.float32)
    outs = pl.pallas_call(
        functools.partial(mix_kernel, count, zs),
        out_shape=[piece] * zs + [act] * 2,
        in_specs=[VMEM] * (count + 1),
        out_specs=[VMEM] * (zs + 2),
        scratch_shapes=[pltpu.VMEM((rows, width), jnp.float32)],
        compiler_params=PARAMS,
        cost_estimate=pl.CostEstimate(
            flops=6 * rows * half * width,
            bytes_accessed=8 * rows * half + 4 * half * width,
            transcendentals=0,
        ),
        name="mix",
    )(*inputs, cols)
    return outs[:zs], outs[zs:]


def pack_kernel(side, zs, moves, *refs):
    total, outs = refs[len(moves) * zs], refs[len(moves) * zs + 1 :]
    rows, columns = total.shape
    head = rows // side
    part, width = head // 2, columns // side // 2
    for k, segments in enumerate(moves):
        got = refs[k * zs : (k + 1) * zs]
        for start, size, to in segments:
            x = got[0][start : start + size]
            for g in got[1:]:
                x = x + g[start : start + size]
            total[to : to + size] = x
    for r in range(side):
        for q in range(side):
            out = outs[r * side + q]
            for e in (0, 1):
                a = r * head + (1 - e) * part
                x = total[a : a + part, 2 * q * width : 2 * (q + 1) * width]
                out[e * part : (e + 1) * part] = jnp.concatenate([x[:, width:], x[:, :width]], 1)


def pack(side, groups, moves):
    zs, columns = len(groups[0]), groups[0][0].shape[1]
    rows = sum(group[0].shape[0] for group in groups)
    block = jax.ShapeDtypeStruct((rows // side, columns // side), jnp.float32)
    outs = pl.pallas_call(
        functools.partial(pack_kernel, side, zs, moves),
        out_shape=[jax.ShapeDtypeStruct((rows, columns), jnp.float32)] + [block] * side**2,
        in_specs=[VMEM] * (len(moves) * zs),
        out_specs=[VMEM] * (1 + side**2),
        compiler_params=PARAMS,
        name="pack",
    )(*[x for group in groups for x in group])
    return outs[0], outs[1:]


def merge_kernel(side, factor, qs, count, *refs):
    out = refs[-1]
    first = 0
    for c in range(count):
        total, *got = refs[c * (1 + side * len(qs)) : (c + 1) * (1 + side * len(qs))]
        head, width = got[0].shape
        for i, q in enumerate(qs):
            for r in range(side):
                x = total[r * head : (r + 1) * head, q * width : (q + 1) * width]
                x = (x + got[i * side + r][...]) * factor
                out[first + r * head : first + (r + 1) * head, i * width : (i + 1) * width] = x
        first += total.shape[0]


def merge(side, factor, qs, chunks):
    inputs = []
    for total, got in chunks:
        inputs += [total] + [got[(-q % side) * side + -r % side] for q in qs for r in range(side)]
    rows = sum(total.shape[0] for total, _ in chunks)
    columns = chunks[0][0].shape[1] // side * len(qs)
    return pl.pallas_call(
        functools.partial(merge_kernel, side, factor, qs, len(chunks)),
        out_shape=jax.ShapeDtypeStruct((rows, columns), jnp.float32),
        in_specs=[VMEM] * len(inputs),
        out_specs=VMEM,
        compiler_params=PARAMS,
        name="merge",
    )(*inputs)


def term_kernel(zs, spots, groups, begin, *refs):
    got = [refs[c * zs : (c + 1) * zs] for c in range(len(spots))]
    refs = refs[len(spots) * zs :]
    acts = refs[: 2 * groups]
    outs, full = refs[2 * groups : -1], refs[-1]
    columns = full.shape[1]
    width, size = outs[0].shape
    z = lax.axis_index("feat")
    for pieces, segments in zip(got, spots):
        for s in range(zs):
            for at, part, to in segments:
                full[pl.ds(to + (z ^ s) * part, part)] = pieces[s][at : at + part]
    h, l = split(full[...].T)
    both = jnp.concatenate([h, l], 0)
    step = block_of(size, 896)

    @pl.loop(0, size // step)
    def _(i):
        to = pl.ds(pl.multiple_of(i * step, step), step)
        at = pl.ds(pl.multiple_of(begin + i * step, 128), step)
        high = jnp.concatenate([x[:, at] for x in acts[::2]], 0)
        low = jnp.concatenate([x[:, at] for x in acts[1::2]], 0)
        d = dot(both, high)
        total = d[:columns] + (d[columns:] + dot(h, low))
        for o, out in enumerate(outs):
            out[:, to] = total[o * width : (o + 1) * width]


def terms(got, acts, spots, width, low=0, high=None):
    zs, columns = len(got[0]), got[0][0].shape[1]
    half = acts[0][0].shape[1]
    count = columns // width
    rows = sum(act[0].shape[0] for act in acts)
    return pl.pallas_call(
        functools.partial(term_kernel, zs, spots, len(acts), low),
        out_shape=[jax.ShapeDtypeStruct((width, (high or half) - low), jnp.float32)] * count,
        in_specs=[VMEM] * (zs * len(got) + 2 * len(acts)),
        out_specs=[VMEM] * count,
        scratch_shapes=[pltpu.VMEM((rows, columns), jnp.float32)],
        compiler_params=PARAMS,
        cost_estimate=pl.CostEstimate(
            flops=0, bytes_accessed=0, transcendentals=0
        ),
        name="term",
    )(*[x for pieces in got for x in pieces], *[x for act in acts for x in act])


def arrived_kernel(*refs):
    refs[-1][...] = jnp.zeros_like(refs[-1])


def arrived(blocks):
    return pl.pallas_call(
        arrived_kernel,
        out_shape=jax.ShapeDtypeStruct((8, 128), jnp.float32),
        in_specs=[pl.BlockSpec(memory_space=pl.ANY)] * len(blocks),
        out_specs=VMEM,
        compiler_params=PARAMS,
        cost_estimate=pl.CostEstimate(flops=10**10, bytes_accessed=0, transcendentals=0),
        name="arrived",
    )(*blocks)


def join_kernel(sides, low, *refs):
    staged, sems, out = refs[-2], refs[-1], refs[-3]
    core = lax.axis_index("tok") & 1
    half = out.shape[1] // 2
    width, size = staged.shape[1:]
    rows = 16 if width % 16 == 0 else width
    copies = []
    for i in range(0, width, rows):
        first = 0
        for k, count in enumerate(sides):
            whole, *arrivals = refs[first : first + count]
            first += count
            x = whole[i : i + rows, low : low + size]
            for ref in arrivals:
                x = x + ref[i : i + rows]
            staged[k, i : i + rows] = x
            at = pl.multiple_of((core ^ k) * half + low, 128)
            copy = pltpu.make_async_copy(
                staged.at[k, pl.ds(i, rows)],
                out.at[pl.ds(i, rows), pl.ds(at, size)],
                sems.at[len(copies)],
            )
            copy.start()
            copies.append(copy)
    for copy in copies:
        copy.wait()


def join(own, other, low, mark, before=()):
    width, half = own[0].shape
    size = own[1].shape[1]
    inputs = [*own, *other]
    rows = 16 if width % 16 == 0 else width
    hbm = pl.BlockSpec(memory_space=pl.ANY)
    return pl.pallas_call(
        functools.partial(join_kernel, (len(own), len(other)), low),
        out_shape=jax.ShapeDtypeStruct((width, 2 * half), jnp.float32),
        in_specs=[VMEM] * len(inputs) + [hbm] * (len(mark) + len(before)),
        out_specs=hbm,
        input_output_aliases={len(inputs) + len(mark): 0} if before else {},
        scratch_shapes=[
            pltpu.VMEM((2, width, size), jnp.float32),
            pltpu.SemaphoreType.DMA((2 * width // rows,)),
        ],
        compiler_params=PARAMS,
        name="join",
    )(*inputs, *mark, *before)


def shards(side, calib, weight):
    zs = lax.axis_size("feat")
    tokens = calib.shape[0]
    width = weight.shape[1]
    along, swap = routes(side)
    turns = range(side)
    send = lambda x, pairs: lax.ppermute(x, "tok", pairs)
    across = lambda x, s: lax.ppermute(x, "feat", [(i, i ^ s) for i in range(zs)])
    factor = 1.0 / math.sqrt(tokens * lax.axis_size("tok"))
    unit = 8 * zs if tokens % (8 * zs) == 0 else zs
    late = unit * max(1, tokens // unit * 2 // 5)
    sizes = [tokens - late, late]

    def reduce(group, cols):
        pieces, act = mix(group, cols, zs)
        return list(pieces[:1]) + [across(pieces[s], s) for s in order][::-1], act

    order = range(zs - 1, 0, -1)

    def far(own, other, which):
        got = []
        for r in turns[1:]:
            got.append(send(own, along(side - r, 0, which)))
            got.append(send(other, along(side - r, 1, which)))
        return got

    ((own, other),) = cut(weight.T, [(0, width)])
    close = send(other, along(0, 1, "columns"))
    cols = turn([own, close] + far(own, other, "columns"))
    parts = [own, other]
    for own, other in cut(calib, [(0, sizes[0]), (sizes[0], sizes[1])]):
        parts += [other, own]
    near = []
    for c in (0, 1):
        other, own = parts[2 + 2 * c : 4 + 2 * c]
        near += [own, send(other, along(0, 1, "rows"))]
    hold = lax.optimization_barrier
    last, act = reduce(near, cols)
    acts, groups = [act], [last]
    for other, own in (parts[2:4], parts[4:6]):
        group, groups[-1] = hold((far(own, other, "rows"), groups[-1]))
        last, act = reduce(group, cols)
        acts.append(act)
        groups.append(last)

    part, first = tokens // zs, 2 * tokens
    moves, spots = [[], [], []], []
    for c in (0, 1):
        size = sizes[c] // zs
        for p in range(2 * side):
            at = p * part + c * sizes[0] // zs
            if p < 2:
                start = 2 * c * sizes[0] + p * sizes[c]
                moves[0].append((start // zs, size, at))
            else:
                start = first + (p - 2) * sizes[c]
                moves[c + 1].append(((p - 2) * size, size, at))
            spots.append((at, size, start))
        first += (2 * side - 2) * sizes[c]

    total, payloads = pack(side, groups, moves)
    pairs = [swap(r, q) for r in turns for q in turns]
    chunk = (total, [send(x, pair) for x, pair in zip(payloads, pairs)])

    def spread(mine):
        return [mine] + [across(mine, s) for s in order][::-1]

    away = spread(merge(side, factor, turns[1:], [chunk]))
    here = merge(side, factor, turns[:1], [chunk])
    here, away = hold((here, away))
    half = acts[0][0].shape[1]
    cuts = [(0, half)]
    same, cross = [], []
    for low, high in cuts:
        term = terms([away], acts, [spots], width, low, high)
        same.append([send(term[2 * q - 2], along(q, 0, "results")) for q in turns[1:]])
        cross.append([send(term[2 * q - 1], along(q, 1, "results")) for q in turns[1:]])
        (here, away), term = hold(((here, away), term))
    here = spread(here)
    here, term = hold((here, term))
    mine, near = terms([here], acts, [spots], width)
    near = send(near, along(0, 1, "results"))
    out = ()
    for (low, high), s, c in zip(cuts, same, cross):
        last = high == half
        mark = [arrived([x for part in (same + cross) for x in part])] if last else []
        out = (join([mine] + s, [near] + c, low, mark, out),)
    return out[0]


def solution(mesh):
    side = math.isqrt(mesh.shape["tok"] // 2)

    def step(calib, weight):
        return shards(side, calib, weight)

    return jax.shard_map(
        step,
        mesh=mesh,
        in_specs=(P("tok", "feat"), P("feat", "tok")),
        out_specs=P("tok", "feat"),
        check_vma=False,
    )
```

```python
import functools
import math

import jax
import jax.numpy as jnp
from jax import lax
from jax.experimental import pallas as pl
from jax.experimental.pallas import tpu as pltpu
from jax.sharding import PartitionSpec as P

VMEM = pl.BlockSpec(memory_space=pltpu.VMEM)
PARAMS = pltpu.CompilerParams(vmem_limit_bytes=20 * 2**20)


def routes(side):
    place = lambda a, b, core: ((a % side) * side + b % side) * 2 + core
    every = [(a, b, core) for a in range(side) for b in range(side) for core in (0, 1)]

    def along(step, cross, which):
        pairs = []
        for a, b, core in every:
            moves_a = {"rows": core ^ cross == 1, "columns": core ^ cross == 0, "results": core == 0}
            there = (a + step, b) if moves_a[which] else (a, b + step)
            pairs.append((place(a, b, core), place(*there, core ^ cross)))
        return pairs

    def swap(row, column):
        pairs = []
        for a, b, core in every:
            there = (a + column, b + row) if core == 0 else (a + row, b + column)
            pairs.append((place(a, b, core), place(*there, 1 - core)))
        return pairs

    return along, swap


def split(x):
    high = x.astype(jnp.bfloat16)
    return high, (x - high.astype(jnp.float32)).astype(jnp.bfloat16)


def dot(left, right):
    return jnp.dot(left, right, preferred_element_type=jnp.float32)


def block_of(size, most):
    return next(b for b in range(most, 0, -128) if size % b == 0)


def cut_kernel(cuts, source, *refs):
    outs, sems = refs[:-1], refs[-1]
    half = source.shape[1] // 2
    core = lax.axis_index("tok") & 1
    copies = []
    for start, size in cuts:
        for first in (1 - core, core):
            at = pl.ds(pl.multiple_of(first * half, half), half)
            k = len(copies)
            copy = pltpu.make_async_copy(
                source.at[pl.ds(start, size), at], outs[k], sems.at[k]
            )
            copy.start()
            copies.append(copy)
    for copy in copies:
        copy.wait()


def cut(source, cuts):
    half = source.shape[1] // 2
    outs = pl.pallas_call(
        functools.partial(cut_kernel, cuts),
        out_shape=[jax.ShapeDtypeStruct((n, half), jnp.float32) for _, n in cuts for _ in range(2)],
        in_specs=[pl.BlockSpec(memory_space=pl.ANY)],
        out_specs=[VMEM] * (2 * len(cuts)),
        scratch_shapes=[pltpu.SemaphoreType.DMA((2 * len(cuts),))],
        compiler_params=PARAMS,
        name="cut",
    )(source)
    return [(outs[2 * i + 1], outs[2 * i]) for i in range(len(cuts))]


def turn_kernel(*refs):
    inputs, out = refs[:-1], refs[-1]
    width, half = inputs[0].shape
    columns = width * len(inputs)
    step = block_of(half, 512)

    @pl.loop(0, half // step)
    def _(i):
        at = pl.ds(pl.multiple_of(i * step, step), step)
        x = jnp.concatenate([ref[:, at] for ref in inputs], 0).T
        out[at, :columns], out[at, columns:] = split(x)


def turn(inputs):
    width, half = inputs[0].shape
    return pl.pallas_call(
        turn_kernel,
        out_shape=jax.ShapeDtypeStruct((half, 2 * width * len(inputs)), jnp.bfloat16),
        in_specs=[VMEM] * len(inputs),
        out_specs=VMEM,
        compiler_params=PARAMS,
        name="turn",
    )(*inputs)


def mix_kernel(count, zs, *refs):
    inputs, cols = refs[:count], refs[count]
    pieces, (high, low), acc = refs[count + 1 : count + 1 + zs], refs[-3:-1], refs[-1]
    half = inputs[0].shape[1]
    width = acc.shape[1]
    z = lax.axis_index("feat")
    step = block_of(half, 1024)
    acc[...] = jnp.zeros(acc.shape, jnp.float32)

    @pl.loop(0, half // step)
    def _(i):
        at = pl.ds(pl.multiple_of(i * step, step), step)
        h, l = split(jnp.concatenate([x[:, at] for x in inputs], 0))
        high[:, at], low[:, at] = h, l
        w = cols[at, :]
        d = dot(h, w)
        acc[...] += d[:, :width] + (d[:, width:] + dot(l, w[:, :width]))

    first = 0
    for x in inputs:
        part = x.shape[0] // zs
        for s in range(zs):
            pieces[s][first // zs : first // zs + part] = acc[pl.ds(first + (z ^ s) * part, part)]
        first += x.shape[0]


def mix(inputs, cols, zs):
    count, half = len(inputs), inputs[0].shape[1]
    rows = sum(x.shape[0] for x in inputs)
    width = cols.shape[1] // 2
    act = jax.ShapeDtypeStruct((rows, half), jnp.bfloat16)
    piece = jax.ShapeDtypeStruct((rows // zs, width), jnp.float32)
    outs = pl.pallas_call(
        functools.partial(mix_kernel, count, zs),
        out_shape=[piece] * zs + [act] * 2,
        in_specs=[VMEM] * (count + 1),
        out_specs=[VMEM] * (zs + 2),
        scratch_shapes=[pltpu.VMEM((rows, width), jnp.float32)],
        compiler_params=PARAMS,
        cost_estimate=pl.CostEstimate(
            flops=6 * rows * half * width,
            bytes_accessed=8 * rows * half + 4 * half * width,
            transcendentals=0,
        ),
        name="mix",
    )(*inputs, cols)
    return outs[:zs], outs[zs:]


def pack_kernel(side, zs, moves, *refs):
    total, outs = refs[len(moves) * zs], refs[len(moves) * zs + 1 :]
    rows, columns = total.shape
    head = rows // side
    part, width = head // 2, columns // side // 2
    for k, segments in enumerate(moves):
        got = refs[k * zs : (k + 1) * zs]
        for start, size, to in segments:
            x = got[0][start : start + size]
            for g in got[1:]:
                x = x + g[start : start + size]
            total[to : to + size] = x
    for r in range(side):
        for q in range(side):
            out = outs[r * side + q]
            for e in (0, 1):
                a = r * head + (1 - e) * part
                x = total[a : a + part, 2 * q * width : 2 * (q + 1) * width]
                out[e * part : (e + 1) * part] = jnp.concatenate([x[:, width:], x[:, :width]], 1)


def pack(side, groups, moves):
    zs, columns = len(groups[0]), groups[0][0].shape[1]
    rows = sum(group[0].shape[0] for group in groups)
    block = jax.ShapeDtypeStruct((rows // side, columns // side), jnp.float32)
    outs = pl.pallas_call(
        functools.partial(pack_kernel, side, zs, moves),
        out_shape=[jax.ShapeDtypeStruct((rows, columns), jnp.float32)] + [block] * side**2,
        in_specs=[VMEM] * (len(moves) * zs),
        out_specs=[VMEM] * (1 + side**2),
        compiler_params=PARAMS,
        name="pack",
    )(*[x for group in groups for x in group])
    return outs[0], outs[1:]


def merge_kernel(side, factor, qs, count, *refs):
    out = refs[-1]
    first = 0
    for c in range(count):
        total, *got = refs[c * (1 + side * len(qs)) : (c + 1) * (1 + side * len(qs))]
        head, width = got[0].shape
        for i, q in enumerate(qs):
            for r in range(side):
                x = total[r * head : (r + 1) * head, q * width : (q + 1) * width]
                x = (x + got[i * side + r][...]) * factor
                out[first + r * head : first + (r + 1) * head, i * width : (i + 1) * width] = x
        first += total.shape[0]


def merge(side, factor, qs, chunks):
    inputs = []
    for total, got in chunks:
        inputs += [total] + [got[(-q % side) * side + -r % side] for q in qs for r in range(side)]
    rows = sum(total.shape[0] for total, _ in chunks)
    columns = chunks[0][0].shape[1] // side * len(qs)
    return pl.pallas_call(
        functools.partial(merge_kernel, side, factor, qs, len(chunks)),
        out_shape=jax.ShapeDtypeStruct((rows, columns), jnp.float32),
        in_specs=[VMEM] * len(inputs),
        out_specs=VMEM,
        compiler_params=PARAMS,
        name="merge",
    )(*inputs)


def term_kernel(zs, spots, groups, left, *refs):
    got = [refs[c * zs : (c + 1) * zs] for c in range(len(spots))]
    refs = refs[len(spots) * zs :]
    acts = refs[: 2 * groups]
    outs, full = refs[2 * groups : -1], refs[-1]
    columns = full.shape[1]
    width, size = outs[0].shape
    z = lax.axis_index("feat")
    for pieces, segments in zip(got, spots):
        for s in range(zs):
            for at, part, to in segments:
                full[pl.ds(to + (z ^ s) * part, part)] = pieces[s][at : at + part, left : left + columns]
    h, l = split(full[...].T)
    both = jnp.concatenate([h, l], 0)
    step = block_of(size, 896)

    @pl.loop(0, size // step)
    def _(i):
        to = pl.ds(pl.multiple_of(i * step, step), step)
        at = pl.ds(pl.multiple_of(i * step, 128), step)
        high = jnp.concatenate([x[:, at] for x in acts[::2]], 0)
        low = jnp.concatenate([x[:, at] for x in acts[1::2]], 0)
        d = dot(both, high)
        total = d[:columns] + (d[columns:] + dot(h, low))
        for o, out in enumerate(outs):
            out[:, to] = total[o * width : (o + 1) * width]


def terms(got, acts, spots, width, left, columns):
    zs = len(got[0])
    half = acts[0][0].shape[1]
    count = columns // width
    rows = sum(act[0].shape[0] for act in acts)
    return pl.pallas_call(
        functools.partial(term_kernel, zs, spots, len(acts), left),
        out_shape=[jax.ShapeDtypeStruct((width, half), jnp.float32)] * count,
        in_specs=[VMEM] * (zs * len(got) + 2 * len(acts)),
        out_specs=[VMEM] * count,
        scratch_shapes=[pltpu.VMEM((rows, columns), jnp.float32)],
        compiler_params=PARAMS,
        cost_estimate=pl.CostEstimate(
            flops=0, bytes_accessed=0, transcendentals=0
        ),
        name="term",
    )(*[x for pieces in got for x in pieces], *[x for act in acts for x in act])


def arrived_kernel(*refs):
    refs[-1][...] = jnp.zeros_like(refs[-1])


def arrived(blocks):
    return pl.pallas_call(
        arrived_kernel,
        out_shape=jax.ShapeDtypeStruct((8, 128), jnp.float32),
        in_specs=[pl.BlockSpec(memory_space=pl.ANY)] * len(blocks),
        out_specs=VMEM,
        compiler_params=PARAMS,
        cost_estimate=pl.CostEstimate(flops=10**10, bytes_accessed=0, transcendentals=0),
        name="arrived",
    )(*blocks)


def join_kernel(sides, low, *refs):
    staged, sems, out = refs[-2], refs[-1], refs[-3]
    core = lax.axis_index("tok") & 1
    half = out.shape[1] // 2
    width, size = staged.shape[1:]
    rows = 16 if width % 16 == 0 else width
    copies = []
    for i in range(0, width, rows):
        first = 0
        for k, count in enumerate(sides):
            whole, *arrivals = refs[first : first + count]
            first += count
            x = whole[i : i + rows, low : low + size]
            for ref in arrivals:
                x = x + ref[i : i + rows]
            staged[k, i : i + rows] = x
            at = pl.multiple_of((core ^ k) * half + low, 128)
            copy = pltpu.make_async_copy(
                staged.at[k, pl.ds(i, rows)],
                out.at[pl.ds(i, rows), pl.ds(at, size)],
                sems.at[len(copies)],
            )
            copy.start()
            copies.append(copy)
    for copy in copies:
        copy.wait()


def join(own, other, low, mark, before=()):
    width, half = own[0].shape
    size = own[1].shape[1]
    inputs = [*own, *other]
    rows = 16 if width % 16 == 0 else width
    hbm = pl.BlockSpec(memory_space=pl.ANY)
    return pl.pallas_call(
        functools.partial(join_kernel, (len(own), len(other)), low),
        out_shape=jax.ShapeDtypeStruct((width, 2 * half), jnp.float32),
        in_specs=[VMEM] * len(inputs) + [hbm] * (len(mark) + len(before)),
        out_specs=hbm,
        input_output_aliases={len(inputs) + len(mark): 0} if before else {},
        scratch_shapes=[
            pltpu.VMEM((2, width, size), jnp.float32),
            pltpu.SemaphoreType.DMA((2 * width // rows,)),
        ],
        compiler_params=PARAMS,
        name="join",
    )(*inputs, *mark, *before)


def shards(side, calib, weight):
    zs = lax.axis_size("feat")
    tokens = calib.shape[0]
    width = weight.shape[1]
    along, swap = routes(side)
    turns = range(side)
    send = lambda x, pairs: lax.ppermute(x, "tok", pairs)
    across = lambda x, s: lax.ppermute(x, "feat", [(i, i ^ s) for i in range(zs)])
    factor = 1.0 / math.sqrt(tokens * lax.axis_size("tok"))
    unit = 8 * zs if tokens % (8 * zs) == 0 else zs
    late = unit * max(1, tokens // unit * 2 // 5)
    sizes = [tokens - late, late]

    def reduce(group, cols):
        pieces, act = mix(group, cols, zs)
        return list(pieces[:1]) + [across(pieces[s], s) for s in order], act

    order = sorted(range(1, zs), key=lambda s: s ^ (zs // 2))

    def far(own, other, which):
        got = []
        for r in turns[1:]:
            got.append(send(own, along(side - r, 0, which)))
            got.append(send(other, along(side - r, 1, which)))
        return got

    ((own, other),) = cut(weight.T, [(0, width)])
    close = send(other, along(0, 1, "columns"))
    cols = turn([own, close] + far(own, other, "columns"))
    parts = [own, other]
    for own, other in cut(calib, [(0, sizes[0]), (sizes[0], sizes[1])]):
        parts += [other, own]
    near = []
    for c in (0, 1):
        other, own = parts[2 + 2 * c : 4 + 2 * c]
        near += [own, send(other, along(0, 1, "rows"))]
    hold = lax.optimization_barrier
    last, act = reduce(near, cols)
    acts, groups = [act], [last]
    for other, own in (parts[2:4], parts[4:6]):
        group, groups[-1] = hold((far(own, other, "rows"), groups[-1]))
        last, act = reduce(group, cols)
        acts.append(act)
        groups.append(last)

    part, first = tokens // zs, 2 * tokens
    moves, spots = [[], [], []], []
    for c in (0, 1):
        size = sizes[c] // zs
        for p in range(2 * side):
            at = p * part + c * sizes[0] // zs
            if p < 2:
                start = 2 * c * sizes[0] + p * sizes[c]
                moves[0].append((start // zs, size, at))
            else:
                start = first + (p - 2) * sizes[c]
                moves[c + 1].append(((p - 2) * size, size, at))
            spots.append((at, size, start))
        first += (2 * side - 2) * sizes[c]

    total, payloads = pack(side, groups, moves)
    pairs = [swap(r, q) for r in turns for q in turns]
    chunk = (total, [send(x, pair) for x, pair in zip(payloads, pairs)])

    def spread(mine):
        return [mine] + [x for _, x in sorted([(s, across(mine, s)) for s in order], key=lambda t: t[0])]

    away = spread(merge(side, factor, turns[1:], [chunk]))
    here = merge(side, factor, turns[:1], [chunk])
    here, away = hold((here, away))
    half = acts[0][0].shape[1]
    same, cross = [], []
    for q in turns[1:]:
        for core, results in ((1, cross), (0, same)):
            left = width * (2 * q - 2 + core)
            (term,) = terms([away], acts, [spots], width, left, width)
            results.append(send(term, along(q, core, "results")))
            (here, away), term = hold(((here, away), term))
    here = spread(here)
    here, term = hold((here, term))
    mine, near = terms([here], acts, [spots], width, 0, 2 * width)
    near = send(near, along(0, 1, "results"))
    return join([mine] + same, [near] + cross, 0, [arrived(same + [arrived(cross)])])


def solution(mesh):
    side = math.isqrt(mesh.shape["tok"] // 2)

    def step(calib, weight):
        return shards(side, calib, weight)

    return jax.shard_map(
        step,
        mesh=mesh,
        in_specs=(P("tok", "feat"), P("feat", "tok")),
        out_specs=P("tok", "feat"),
        check_vma=False,
    )
```

```python
import functools
import math

import jax
import jax.numpy as jnp
from jax import lax
from jax.experimental import pallas as pl
from jax.experimental.pallas import tpu as pltpu
from jax.sharding import PartitionSpec as P

VMEM = pl.BlockSpec(memory_space=pltpu.VMEM)
PARAMS = pltpu.CompilerParams(vmem_limit_bytes=20 * 2**20)


def routes(side):
    place = lambda a, b, core: ((a % side) * side + b % side) * 2 + core
    every = [(a, b, core) for a in range(side) for b in range(side) for core in (0, 1)]

    def along(step, cross, which):
        pairs = []
        for a, b, core in every:
            moves_a = {"rows": core ^ cross == 1, "columns": core ^ cross == 0, "results": core == 0}
            there = (a + step, b) if moves_a[which] else (a, b + step)
            pairs.append((place(a, b, core), place(*there, core ^ cross)))
        return pairs

    def swap(row, column):
        pairs = []
        for a, b, core in every:
            there = (a + column, b + row) if core == 0 else (a + row, b + column)
            pairs.append((place(a, b, core), place(*there, 1 - core)))
        return pairs

    return along, swap


def split(x):
    high = x.astype(jnp.bfloat16)
    return high, (x - high.astype(jnp.float32)).astype(jnp.bfloat16)


def dot(left, right):
    return jnp.dot(left, right, preferred_element_type=jnp.float32)


def block_of(size, most):
    return next(b for b in range(most, 0, -128) if size % b == 0)


def cut_kernel(cuts, source, *refs):
    outs, sems = refs[:-1], refs[-1]
    half = source.shape[1] // 2
    core = lax.axis_index("tok") & 1
    copies = []
    for start, size in cuts:
        for first in (1 - core, core):
            at = pl.ds(pl.multiple_of(first * half, half), half)
            k = len(copies)
            copy = pltpu.make_async_copy(
                source.at[pl.ds(start, size), at], outs[k], sems.at[k]
            )
            copy.start()
            copies.append(copy)
    for copy in copies:
        copy.wait()


def cut(source, cuts):
    half = source.shape[1] // 2
    outs = pl.pallas_call(
        functools.partial(cut_kernel, cuts),
        out_shape=[jax.ShapeDtypeStruct((n, half), jnp.float32) for _, n in cuts for _ in range(2)],
        in_specs=[pl.BlockSpec(memory_space=pl.ANY)],
        out_specs=[VMEM] * (2 * len(cuts)),
        scratch_shapes=[pltpu.SemaphoreType.DMA((2 * len(cuts),))],
        compiler_params=PARAMS,
        name="cut",
    )(source)
    return [(outs[2 * i + 1], outs[2 * i]) for i in range(len(cuts))]


def turn_kernel(*refs):
    inputs, out = refs[:-1], refs[-1]
    width, half = inputs[0].shape
    columns = width * len(inputs)
    step = block_of(half, 512)

    @pl.loop(0, half // step)
    def _(i):
        at = pl.ds(pl.multiple_of(i * step, step), step)
        x = jnp.concatenate([ref[:, at] for ref in inputs], 0).T
        out[at, :columns], out[at, columns:] = split(x)


def turn(inputs):
    width, half = inputs[0].shape
    return pl.pallas_call(
        turn_kernel,
        out_shape=jax.ShapeDtypeStruct((half, 2 * width * len(inputs)), jnp.bfloat16),
        in_specs=[VMEM] * len(inputs),
        out_specs=VMEM,
        compiler_params=PARAMS,
        name="turn",
    )(*inputs)


def mix_kernel(count, zs, *refs):
    inputs, cols = refs[:count], refs[count]
    pieces, (high, low), acc = refs[count + 1 : count + 1 + zs], refs[-3:-1], refs[-1]
    half = inputs[0].shape[1]
    width = acc.shape[1]
    z = lax.axis_index("feat")
    step = block_of(half, 4096)
    acc[...] = jnp.zeros(acc.shape, jnp.float32)

    @pl.loop(0, half // step)
    def _(i):
        at = pl.ds(pl.multiple_of(i * step, step), step)
        h, l = split(jnp.concatenate([x[:, at] for x in inputs], 0))
        high[:, at], low[:, at] = h, l
        w = cols[at, :]
        d = dot(h, w)
        acc[...] += d[:, :width] + (d[:, width:] + dot(l, w[:, :width]))

    first = 0
    for x in inputs:
        part = x.shape[0] // zs
        for s in range(zs):
            pieces[s][first // zs : first // zs + part] = acc[pl.ds(first + (z ^ s) * part, part)]
        first += x.shape[0]


def mix(inputs, cols, zs):
    count, half = len(inputs), inputs[0].shape[1]
    rows = sum(x.shape[0] for x in inputs)
    width = cols.shape[1] // 2
    act = jax.ShapeDtypeStruct((rows, half), jnp.bfloat16)
    piece = jax.ShapeDtypeStruct((rows // zs, width), jnp.float32)
    outs = pl.pallas_call(
        functools.partial(mix_kernel, count, zs),
        out_shape=[piece] * zs + [act] * 2,
        in_specs=[VMEM] * (count + 1),
        out_specs=[VMEM] * (zs + 2),
        scratch_shapes=[pltpu.VMEM((rows, width), jnp.float32)],
        compiler_params=PARAMS,
        cost_estimate=pl.CostEstimate(
            flops=6 * rows * half * width,
            bytes_accessed=8 * rows * half + 4 * half * width,
            transcendentals=0,
        ),
        name="mix",
    )(*inputs, cols)
    return outs[:zs], outs[zs:]


def pack_kernel(side, zs, moves, *refs):
    total, outs = refs[len(moves) * zs], refs[len(moves) * zs + 1 :]
    rows, columns = total.shape
    head = rows // side
    part, width = head // 2, columns // side // 2
    for k, segments in enumerate(moves):
        got = refs[k * zs : (k + 1) * zs]
        for start, size, to in segments:
            x = got[0][start : start + size]
            for g in got[1:]:
                x = x + g[start : start + size]
            total[to : to + size] = x
    for r in range(side):
        for q in range(side):
            out = outs[r * side + q]
            for e in (0, 1):
                a = r * head + (1 - e) * part
                x = total[a : a + part, 2 * q * width : 2 * (q + 1) * width]
                out[e * part : (e + 1) * part] = jnp.concatenate([x[:, width:], x[:, :width]], 1)


def pack(side, groups, moves):
    zs, columns = len(groups[0]), groups[0][0].shape[1]
    rows = sum(group[0].shape[0] for group in groups)
    block = jax.ShapeDtypeStruct((rows // side, columns // side), jnp.float32)
    outs = pl.pallas_call(
        functools.partial(pack_kernel, side, zs, moves),
        out_shape=[jax.ShapeDtypeStruct((rows, columns), jnp.float32)] + [block] * side**2,
        in_specs=[VMEM] * (len(moves) * zs),
        out_specs=[VMEM] * (1 + side**2),
        compiler_params=PARAMS,
        name="pack",
    )(*[x for group in groups for x in group])
    return outs[0], outs[1:]


def merge_kernel(side, factor, qs, count, *refs):
    out = refs[-1]
    first = 0
    for c in range(count):
        total, *got = refs[c * (1 + side * len(qs)) : (c + 1) * (1 + side * len(qs))]
        head, width = got[0].shape
        for i, q in enumerate(qs):
            for r in range(side):
                x = total[r * head : (r + 1) * head, q * width : (q + 1) * width]
                x = (x + got[i * side + r][...]) * factor
                out[first + r * head : first + (r + 1) * head, i * width : (i + 1) * width] = x
        first += total.shape[0]


def merge(side, factor, qs, chunks):
    inputs = []
    for total, got in chunks:
        inputs += [total] + [got[(-q % side) * side + -r % side] for q in qs for r in range(side)]
    rows = sum(total.shape[0] for total, _ in chunks)
    columns = chunks[0][0].shape[1] // side * len(qs)
    return pl.pallas_call(
        functools.partial(merge_kernel, side, factor, qs, len(chunks)),
        out_shape=jax.ShapeDtypeStruct((rows, columns), jnp.float32),
        in_specs=[VMEM] * len(inputs),
        out_specs=VMEM,
        compiler_params=PARAMS,
        name="merge",
    )(*inputs)


def term_kernel(zs, spots, groups, left, *refs):
    got = [refs[c * zs : (c + 1) * zs] for c in range(len(spots))]
    refs = refs[len(spots) * zs :]
    acts = refs[: 2 * groups]
    outs, full = refs[2 * groups : -1], refs[-1]
    columns = full.shape[1]
    width, size = outs[0].shape
    z = lax.axis_index("feat")
    for pieces, segments in zip(got, spots):
        for s in range(zs):
            for at, part, to in segments:
                full[pl.ds(to + (z ^ s) * part, part)] = pieces[s][at : at + part, left : left + columns]
    h, l = split(full[...].T)
    both = jnp.concatenate([h, l], 0)
    step = block_of(size, 4096)

    @pl.loop(0, size // step)
    def _(i):
        to = pl.ds(pl.multiple_of(i * step, step), step)
        at = pl.ds(pl.multiple_of(i * step, 128), step)
        high = jnp.concatenate([x[:, at] for x in acts[::2]], 0)
        low = jnp.concatenate([x[:, at] for x in acts[1::2]], 0)
        d = dot(both, high)
        total = d[:columns] + (d[columns:] + dot(h, low))
        for o, out in enumerate(outs):
            out[:, to] = total[o * width : (o + 1) * width]


def terms(got, acts, spots, width, left, columns):
    zs = len(got[0])
    half = acts[0][0].shape[1]
    count = columns // width
    rows = sum(act[0].shape[0] for act in acts)
    return pl.pallas_call(
        functools.partial(term_kernel, zs, spots, len(acts), left),
        out_shape=[jax.ShapeDtypeStruct((width, half), jnp.float32)] * count,
        in_specs=[VMEM] * (zs * len(got) + 2 * len(acts)),
        out_specs=[VMEM] * count,
        scratch_shapes=[pltpu.VMEM((rows, columns), jnp.float32)],
        compiler_params=PARAMS,
        cost_estimate=pl.CostEstimate(
            flops=0, bytes_accessed=0, transcendentals=0
        ),
        name="term",
    )(*[x for pieces in got for x in pieces], *[x for act in acts for x in act])


def arrived_kernel(*refs):
    refs[-1][...] = jnp.zeros_like(refs[-1])


def arrived(blocks):
    return pl.pallas_call(
        arrived_kernel,
        out_shape=jax.ShapeDtypeStruct((8, 128), jnp.float32),
        in_specs=[pl.BlockSpec(memory_space=pl.ANY)] * len(blocks),
        out_specs=VMEM,
        compiler_params=PARAMS,
        cost_estimate=pl.CostEstimate(flops=10**10, bytes_accessed=0, transcendentals=0),
        name="arrived",
    )(*blocks)


def join_kernel(sides, low, *refs):
    staged, sems, out = refs[-2], refs[-1], refs[-3]
    core = lax.axis_index("tok") & 1
    half = out.shape[1] // 2
    width, size = staged.shape[1:]
    rows = 16 if width % 16 == 0 else width
    copies = []
    for i in range(0, width, rows):
        first = 0
        for k, count in enumerate(sides):
            whole, *arrivals = refs[first : first + count]
            first += count
            x = whole[i : i + rows, low : low + size]
            for ref in arrivals:
                x = x + ref[i : i + rows]
            staged[k, i : i + rows] = x
            at = pl.multiple_of((core ^ k) * half + low, 128)
            copy = pltpu.make_async_copy(
                staged.at[k, pl.ds(i, rows)],
                out.at[pl.ds(i, rows), pl.ds(at, size)],
                sems.at[len(copies)],
            )
            copy.start()
            copies.append(copy)
    for copy in copies:
        copy.wait()


def join(own, other, low, mark, before=()):
    width, half = own[0].shape
    size = own[1].shape[1]
    inputs = [*own, *other]
    rows = 16 if width % 16 == 0 else width
    hbm = pl.BlockSpec(memory_space=pl.ANY)
    return pl.pallas_call(
        functools.partial(join_kernel, (len(own), len(other)), low),
        out_shape=jax.ShapeDtypeStruct((width, 2 * half), jnp.float32),
        in_specs=[VMEM] * len(inputs) + [hbm] * (len(mark) + len(before)),
        out_specs=hbm,
        input_output_aliases={len(inputs) + len(mark): 0} if before else {},
        scratch_shapes=[
            pltpu.VMEM((2, width, size), jnp.float32),
            pltpu.SemaphoreType.DMA((2 * width // rows,)),
        ],
        compiler_params=PARAMS,
        name="join",
    )(*inputs, *mark, *before)


def shards(side, calib, weight):
    zs = lax.axis_size("feat")
    tokens = calib.shape[0]
    width = weight.shape[1]
    along, swap = routes(side)
    turns = range(side)
    send = lambda x, pairs: lax.ppermute(x, "tok", pairs)
    across = lambda x, s: lax.ppermute(x, "feat", [(i, i ^ s) for i in range(zs)])
    factor = 1.0 / math.sqrt(tokens * lax.axis_size("tok"))
    unit = 8 * zs if tokens % (8 * zs) == 0 else zs
    late = unit * max(1, tokens // unit * 2 // 5)
    sizes = [tokens - late, late]

    def reduce(group, cols):
        pieces, act = mix(group, cols, zs)
        return list(pieces[:1]) + [across(pieces[s], s) for s in order], act

    order = sorted(range(1, zs), key=lambda s: s ^ (zs // 2))

    def far(own, other, which):
        got = []
        for r in turns[1:]:
            got.append(send(own, along(side - r, 0, which)))
            got.append(send(other, along(side - r, 1, which)))
        return got

    ((own, other),) = cut(weight.T, [(0, width)])
    close = send(other, along(0, 1, "columns"))
    cols = turn([own, close] + far(own, other, "columns"))
    parts = [own, other]
    for own, other in cut(calib, [(0, sizes[0]), (sizes[0], sizes[1])]):
        parts += [other, own]
    near = []
    for c in (0, 1):
        other, own = parts[2 + 2 * c : 4 + 2 * c]
        near += [own, send(other, along(0, 1, "rows"))]
    hold = lax.optimization_barrier
    last, act = reduce(near, cols)
    acts, groups = [act], [last]
    for other, own in (parts[2:4], parts[4:6]):
        group, groups[-1] = hold((far(own, other, "rows"), groups[-1]))
        last, act = reduce(group, cols)
        acts.append(act)
        groups.append(last)

    part, first = tokens // zs, 2 * tokens
    moves, spots = [[], [], []], []
    for c in (0, 1):
        size = sizes[c] // zs
        for p in range(2 * side):
            at = p * part + c * sizes[0] // zs
            if p < 2:
                start = 2 * c * sizes[0] + p * sizes[c]
                moves[0].append((start // zs, size, at))
            else:
                start = first + (p - 2) * sizes[c]
                moves[c + 1].append(((p - 2) * size, size, at))
            spots.append((at, size, start))
        first += (2 * side - 2) * sizes[c]

    total, payloads = pack(side, groups, moves)
    pairs = [swap(r, q) for r in turns for q in turns]
    chunk = (total, [send(x, pair) for x, pair in zip(payloads, pairs)])

    def spread(mine):
        return [mine] + [x for _, x in sorted([(s, across(mine, s)) for s in order], key=lambda t: t[0])]

    away = spread(merge(side, factor, turns[1:], [chunk]))
    here = merge(side, factor, turns[:1], [chunk])
    here, away = hold((here, away))
    half = acts[0][0].shape[1]
    same, cross = [], []
    for q in turns[1:]:
        for core, results in ((1, cross), (0, same)):
            left = width * (2 * q - 2 + core)
            (term,) = terms([away], acts, [spots], width, left, width)
            results.append(send(term, along(q, core, "results")))
            (here, away), term = hold(((here, away), term))
    here = spread(here)
    here, term = hold((here, term))
    mine, near = terms([here], acts, [spots], width, 0, 2 * width)
    near = send(near, along(0, 1, "results"))
    return join([mine] + same, [near] + cross, 0, [arrived(same + [arrived(cross)])])


def solution(mesh):
    side = math.isqrt(mesh.shape["tok"] // 2)

    def step(calib, weight):
        return shards(side, calib, weight)

    return jax.shard_map(
        step,
        mesh=mesh,
        in_specs=(P("tok", "feat"), P("feat", "tok")),
        out_specs=P("tok", "feat"),
        check_vma=False,
    )
```

```python
import functools
import math

import jax
import jax.numpy as jnp
from jax import lax
from jax.experimental import pallas as pl
from jax.experimental.pallas import tpu as pltpu
from jax.sharding import PartitionSpec as P

VMEM = pl.BlockSpec(memory_space=pltpu.VMEM)
PARAMS = pltpu.CompilerParams(vmem_limit_bytes=20 * 2**20)


def routes(side):
    place = lambda a, b, core: ((a % side) * side + b % side) * 2 + core
    every = [(a, b, core) for a in range(side) for b in range(side) for core in (0, 1)]

    def along(step, cross, which):
        pairs = []
        for a, b, core in every:
            moves_a = {"rows": core ^ cross == 1, "columns": core ^ cross == 0, "results": core == 0}
            there = (a + step, b) if moves_a[which] else (a, b + step)
            pairs.append((place(a, b, core), place(*there, core ^ cross)))
        return pairs

    def swap(row, column):
        pairs = []
        for a, b, core in every:
            there = (a + column, b + row) if core == 0 else (a + row, b + column)
            pairs.append((place(a, b, core), place(*there, 1 - core)))
        return pairs

    return along, swap


def split(x):
    high = x.astype(jnp.bfloat16)
    return high, (x - high.astype(jnp.float32)).astype(jnp.bfloat16)


def dot(left, right):
    return jnp.dot(left, right, preferred_element_type=jnp.float32)


def block_of(size, most):
    return next(b for b in range(most, 0, -128) if size % b == 0)


def cut_kernel(cuts, source, *refs):
    outs, sems = refs[:-1], refs[-1]
    half = source.shape[1] // 2
    core = lax.axis_index("tok") & 1
    copies = []
    for start, size in cuts:
        for first in (1 - core, core):
            at = pl.ds(pl.multiple_of(first * half, half), half)
            k = len(copies)
            copy = pltpu.make_async_copy(
                source.at[pl.ds(start, size), at], outs[k], sems.at[k]
            )
            copy.start()
            copies.append(copy)
    for copy in copies:
        copy.wait()


def cut(source, cuts):
    half = source.shape[1] // 2
    outs = pl.pallas_call(
        functools.partial(cut_kernel, cuts),
        out_shape=[jax.ShapeDtypeStruct((n, half), jnp.float32) for _, n in cuts for _ in range(2)],
        in_specs=[pl.BlockSpec(memory_space=pl.ANY)],
        out_specs=[VMEM] * (2 * len(cuts)),
        scratch_shapes=[pltpu.SemaphoreType.DMA((2 * len(cuts),))],
        compiler_params=PARAMS,
        name="cut",
    )(source)
    return [(outs[2 * i + 1], outs[2 * i]) for i in range(len(cuts))]


def turn_kernel(*refs):
    inputs, out = refs[:-1], refs[-1]
    width, half = inputs[0].shape
    columns = width * len(inputs)
    step = block_of(half, 4096)

    @pl.loop(0, half // step)
    def _(i):
        at = pl.ds(pl.multiple_of(i * step, step), step)
        x = jnp.concatenate([ref[:, at] for ref in inputs], 0).T
        out[at, :columns], out[at, columns:] = split(x)


def turn(inputs):
    width, half = inputs[0].shape
    return pl.pallas_call(
        turn_kernel,
        out_shape=jax.ShapeDtypeStruct((half, 2 * width * len(inputs)), jnp.bfloat16),
        in_specs=[VMEM] * len(inputs),
        out_specs=VMEM,
        compiler_params=PARAMS,
        name="turn",
    )(*inputs)


def mix_kernel(count, zs, *refs):
    inputs, cols = refs[:count], refs[count]
    pieces, (high, low), acc = refs[count + 1 : count + 1 + zs], refs[-3:-1], refs[-1]
    half = inputs[0].shape[1]
    width = acc.shape[1]
    z = lax.axis_index("feat")
    step = block_of(half, 4096)
    acc[...] = jnp.zeros(acc.shape, jnp.float32)

    @pl.loop(0, half // step)
    def _(i):
        at = pl.ds(pl.multiple_of(i * step, step), step)
        h, l = split(jnp.concatenate([x[:, at] for x in inputs], 0))
        high[:, at], low[:, at] = h, l
        w = cols[at, :]
        d = dot(h, w)
        acc[...] += d[:, :width] + (d[:, width:] + dot(l, w[:, :width]))

    first = 0
    for x in inputs:
        part = x.shape[0] // zs
        for s in range(zs):
            pieces[s][first // zs : first // zs + part] = acc[pl.ds(first + (z ^ s) * part, part)]
        first += x.shape[0]


def mix(inputs, cols, zs):
    count, half = len(inputs), inputs[0].shape[1]
    rows = sum(x.shape[0] for x in inputs)
    width = cols.shape[1] // 2
    act = jax.ShapeDtypeStruct((rows, half), jnp.bfloat16)
    piece = jax.ShapeDtypeStruct((rows // zs, width), jnp.float32)
    outs = pl.pallas_call(
        functools.partial(mix_kernel, count, zs),
        out_shape=[piece] * zs + [act] * 2,
        in_specs=[VMEM] * (count + 1),
        out_specs=[VMEM] * (zs + 2),
        scratch_shapes=[pltpu.VMEM((rows, width), jnp.float32)],
        compiler_params=PARAMS,
        cost_estimate=pl.CostEstimate(
            flops=6 * rows * half * width,
            bytes_accessed=8 * rows * half + 4 * half * width,
            transcendentals=0,
        ),
        name="mix",
    )(*inputs, cols)
    return outs[:zs], outs[zs:]


def pack_kernel(side, zs, moves, *refs):
    total, outs = refs[len(moves) * zs], refs[len(moves) * zs + 1 :]
    rows, columns = total.shape
    head = rows // side
    part, width = head // 2, columns // side // 2
    for k, segments in enumerate(moves):
        got = refs[k * zs : (k + 1) * zs]
        for start, size, to in segments:
            x = got[0][start : start + size]
            for g in got[1:]:
                x = x + g[start : start + size]
            total[to : to + size] = x
    for r in range(side):
        for q in range(side):
            out = outs[r * side + q]
            for e in (0, 1):
                a = r * head + (1 - e) * part
                x = total[a : a + part, 2 * q * width : 2 * (q + 1) * width]
                out[e * part : (e + 1) * part] = jnp.concatenate([x[:, width:], x[:, :width]], 1)


def pack(side, groups, moves):
    zs, columns = len(groups[0]), groups[0][0].shape[1]
    rows = sum(group[0].shape[0] for group in groups)
    block = jax.ShapeDtypeStruct((rows // side, columns // side), jnp.float32)
    outs = pl.pallas_call(
        functools.partial(pack_kernel, side, zs, moves),
        out_shape=[jax.ShapeDtypeStruct((rows, columns), jnp.float32)] + [block] * side**2,
        in_specs=[VMEM] * (len(moves) * zs),
        out_specs=[VMEM] * (1 + side**2),
        compiler_params=PARAMS,
        name="pack",
    )(*[x for group in groups for x in group])
    return outs[0], outs[1:]


def merge_kernel(side, factor, qs, count, *refs):
    out = refs[-1]
    first = 0
    for c in range(count):
        total, *got = refs[c * (1 + side * len(qs)) : (c + 1) * (1 + side * len(qs))]
        head, width = got[0].shape
        for i, q in enumerate(qs):
            for r in range(side):
                x = total[r * head : (r + 1) * head, q * width : (q + 1) * width]
                x = (x + got[i * side + r][...]) * factor
                out[first + r * head : first + (r + 1) * head, i * width : (i + 1) * width] = x
        first += total.shape[0]


def merge(side, factor, qs, chunks):
    inputs = []
    for total, got in chunks:
        inputs += [total] + [got[(-q % side) * side + -r % side] for q in qs for r in range(side)]
    rows = sum(total.shape[0] for total, _ in chunks)
    columns = chunks[0][0].shape[1] // side * len(qs)
    return pl.pallas_call(
        functools.partial(merge_kernel, side, factor, qs, len(chunks)),
        out_shape=jax.ShapeDtypeStruct((rows, columns), jnp.float32),
        in_specs=[VMEM] * len(inputs),
        out_specs=VMEM,
        compiler_params=PARAMS,
        name="merge",
    )(*inputs)


def term_kernel(zs, spots, groups, left, *refs):
    got = [refs[c * zs : (c + 1) * zs] for c in range(len(spots))]
    refs = refs[len(spots) * zs :]
    acts = refs[: 2 * groups]
    outs, full = refs[2 * groups : -1], refs[-1]
    columns = full.shape[1]
    width, size = outs[0].shape
    z = lax.axis_index("feat")
    for pieces, segments in zip(got, spots):
        for s in range(zs):
            for at, part, to in segments:
                full[pl.ds(to + (z ^ s) * part, part)] = pieces[s][at : at + part, left : left + columns]
    h, l = split(full[...].T)
    both = jnp.concatenate([h, l], 0)
    step = block_of(size, 4096)

    @pl.loop(0, size // step)
    def _(i):
        to = pl.ds(pl.multiple_of(i * step, step), step)
        at = pl.ds(pl.multiple_of(i * step, 128), step)
        high = jnp.concatenate([x[:, at] for x in acts[::2]], 0)
        low = jnp.concatenate([x[:, at] for x in acts[1::2]], 0)
        d = dot(both, high)
        total = d[:columns] + (d[columns:] + dot(h, low))
        for o, out in enumerate(outs):
            out[:, to] = total[o * width : (o + 1) * width]


def terms(got, acts, spots, width, left, columns):
    zs = len(got[0])
    half = acts[0][0].shape[1]
    count = columns // width
    rows = sum(act[0].shape[0] for act in acts)
    return pl.pallas_call(
        functools.partial(term_kernel, zs, spots, len(acts), left),
        out_shape=[jax.ShapeDtypeStruct((width, half), jnp.float32)] * count,
        in_specs=[VMEM] * (zs * len(got) + 2 * len(acts)),
        out_specs=[VMEM] * count,
        scratch_shapes=[pltpu.VMEM((rows, columns), jnp.float32)],
        compiler_params=PARAMS,
        cost_estimate=pl.CostEstimate(
            flops=0, bytes_accessed=0, transcendentals=0
        ),
        name="term",
    )(*[x for pieces in got for x in pieces], *[x for act in acts for x in act])


def arrived_kernel(*refs):
    refs[-1][...] = jnp.zeros_like(refs[-1])


def arrived(blocks):
    return pl.pallas_call(
        arrived_kernel,
        out_shape=jax.ShapeDtypeStruct((8, 128), jnp.float32),
        in_specs=[pl.BlockSpec(memory_space=pl.ANY)] * len(blocks),
        out_specs=VMEM,
        compiler_params=PARAMS,
        cost_estimate=pl.CostEstimate(flops=10**10, bytes_accessed=0, transcendentals=0),
        name="arrived",
    )(*blocks)


def join_kernel(sides, low, *refs):
    staged, sems, out = refs[-2], refs[-1], refs[-3]
    core = lax.axis_index("tok") & 1
    half = out.shape[1] // 2
    width, size = staged.shape[1:]
    rows = 32 if width % 32 == 0 else width
    copies = []
    for i in range(0, width, rows):
        first = 0
        for k, count in enumerate(sides):
            whole, *arrivals = refs[first : first + count]
            first += count
            x = whole[i : i + rows, low : low + size]
            for ref in arrivals:
                x = x + ref[i : i + rows]
            staged[k, i : i + rows] = x
            at = pl.multiple_of((core ^ k) * half + low, 128)
            copy = pltpu.make_async_copy(
                staged.at[k, pl.ds(i, rows)],
                out.at[pl.ds(i, rows), pl.ds(at, size)],
                sems.at[len(copies)],
            )
            copy.start()
            copies.append(copy)
    for copy in copies:
        copy.wait()


def join(own, other, low, mark, before=()):
    width, half = own[0].shape
    size = own[1].shape[1]
    inputs = [*own, *other]
    rows = 32 if width % 32 == 0 else width
    hbm = pl.BlockSpec(memory_space=pl.ANY)
    return pl.pallas_call(
        functools.partial(join_kernel, (len(own), len(other)), low),
        out_shape=jax.ShapeDtypeStruct((width, 2 * half), jnp.float32),
        in_specs=[VMEM] * len(inputs) + [hbm] * (len(mark) + len(before)),
        out_specs=hbm,
        input_output_aliases={len(inputs) + len(mark): 0} if before else {},
        scratch_shapes=[
            pltpu.VMEM((2, width, size), jnp.float32),
            pltpu.SemaphoreType.DMA((2 * width // rows,)),
        ],
        compiler_params=PARAMS,
        name="join",
    )(*inputs, *mark, *before)


def shards(side, calib, weight):
    zs = lax.axis_size("feat")
    tokens = calib.shape[0]
    width = weight.shape[1]
    along, swap = routes(side)
    turns = range(side)
    send = lambda x, pairs: lax.ppermute(x, "tok", pairs)
    across = lambda x, s: lax.ppermute(x, "feat", [(i, i ^ s) for i in range(zs)])
    factor = 1.0 / math.sqrt(tokens * lax.axis_size("tok"))
    unit = 8 * zs if tokens % (8 * zs) == 0 else zs
    late = unit * max(1, tokens // unit * 2 // 5)
    sizes = [tokens - late, late]

    def reduce(group, cols):
        pieces, act = mix(group, cols, zs)
        return list(pieces[:1]) + [across(pieces[s], s) for s in order], act

    order = sorted(range(1, zs), key=lambda s: s ^ (zs // 2))

    def far(own, other, which):
        got = []
        for r in turns[1:]:
            got.append(send(own, along(side - r, 0, which)))
            got.append(send(other, along(side - r, 1, which)))
        return got

    ((own, other),) = cut(weight.T, [(0, width)])
    close = send(other, along(0, 1, "columns"))
    cols = turn([own, close] + far(own, other, "columns"))
    parts = [own, other]
    for own, other in cut(calib, [(0, sizes[0]), (sizes[0], sizes[1])]):
        parts += [other, own]
    near = []
    for c in (0, 1):
        other, own = parts[2 + 2 * c : 4 + 2 * c]
        near += [own, send(other, along(0, 1, "rows"))]
    hold = lax.optimization_barrier
    last, act = reduce(near, cols)
    acts, groups = [act], [last]
    for other, own in (parts[2:4], parts[4:6]):
        group, groups[-1] = hold((far(own, other, "rows"), groups[-1]))
        last, act = reduce(group, cols)
        acts.append(act)
        groups.append(last)

    part, first = tokens // zs, 2 * tokens
    moves, spots = [[], [], []], []
    for c in (0, 1):
        size = sizes[c] // zs
        for p in range(2 * side):
            at = p * part + c * sizes[0] // zs
            if p < 2:
                start = 2 * c * sizes[0] + p * sizes[c]
                moves[0].append((start // zs, size, at))
            else:
                start = first + (p - 2) * sizes[c]
                moves[c + 1].append(((p - 2) * size, size, at))
            spots.append((at, size, start))
        first += (2 * side - 2) * sizes[c]

    total, payloads = pack(side, groups, moves)
    pairs = [swap(r, q) for r in turns for q in turns]
    chunk = (total, [send(x, pair) for x, pair in zip(payloads, pairs)])

    def spread(mine):
        return [mine] + [x for _, x in sorted([(s, across(mine, s)) for s in order], key=lambda t: t[0])]

    away = spread(merge(side, factor, turns[1:], [chunk]))
    here = merge(side, factor, turns[:1], [chunk])
    here, away = hold((here, away))
    half = acts[0][0].shape[1]
    same, cross = [], []
    for q in turns[1:]:
        for core, results in ((1, cross), (0, same)):
            left = width * (2 * q - 2 + core)
            (term,) = terms([away], acts, [spots], width, left, width)
            results.append(send(term, along(q, core, "results")))
            (here, away), term = hold(((here, away), term))
    here = spread(here)
    here, term = hold((here, term))
    mine, near = terms([here], acts, [spots], width, 0, 2 * width)
    near = send(near, along(0, 1, "results"))
    return join([mine] + same, [near] + cross, 0, [arrived(same + [arrived(cross)])])


def solution(mesh):
    side = math.isqrt(mesh.shape["tok"] // 2)

    def step(calib, weight):
        return shards(side, calib, weight)

    return jax.shard_map(
        step,
        mesh=mesh,
        in_specs=(P("tok", "feat"), P("feat", "tok")),
        out_specs=P("tok", "feat"),
        check_vma=False,
    )
```
